128 devices in a mesh: node: 16 (over y, z_hi, core), local: 8 (over x, z_lo).
Axes of the slice: x: 4, y: 4, z: 4 (z_hi: 2, z_lo: 2; z = z_hi * 2 + z_lo), core: 2. Of those that a mesh axis runs over, the one named last changes fastest.
Arguments:
- inputs: bfloat16 [2, 8192, 6144], P(None, ('node', 'local')), may hold values from -24 to 24
- weight: bfloat16 [6144, 6144], P('node', 'local'), may hold values from -0.078125 to 0.078125
- cotangent: bfloat16 [2, 8192, 6144], P(None, 'node', 'local'), may hold values from -6 to 6
Outputs:
- output: bfloat16 [2, 8192, 6144], P(None, 'node', 'local')
- input_grad: bfloat16 [2, 8192, 6144], P(None, ('node', 'local'))
- weight_grad: bfloat16 [6144, 6144], P('node', 'local')
The draws below stay inside these ranges and needn't reach their ends.
All inputs are finite; a program needn't handle non-finite values.
Results may differ from the reference program's by a relative error of at most 0.017.
Values may be sent and summed in bfloat16 or wider, within the bound.
A program may use at most 192 MiB of HBM per device.

```python
import math
import jax
import jax.numpy as jnp
from jax import lax

DIN = 6144
DOUT = 6144
MB = 2
TOKENS = 8192
N_NODE = 16
N_LOCAL = 8


def spiked(values, key, source, target, shards_of, factor):
    owner, partner = [(jnp.arange(values.shape[dim]) // (values.shape[dim] // shards_of)).reshape([-1 if axis == dim else 1 for axis in range(values.ndim)]) for dim in (source, target)]
    chosen = jax.random.permutation(key, shards_of)[partner]
    strong = (owner == chosen) | (owner == (partner + shards_of // 2) % shards_of)
    return jnp.where(strong, factor * values, values)


def steps_of(own_key, dims, shards, low, largest):
    def one(axis_at, parts):
        draws = jax.random.uniform(jax.random.fold_in(jax.random.fold_in(own_key, 6), axis_at), (parts,), jnp.float32, low / len(shards), largest / len(shards))
        return jnp.repeat(jnp.exp(draws), dims[axis_at] // parts).reshape((-1,) + (1,) * (len(dims) - axis_at - 1))

    gain = one(*shards[0])
    for cut in shards[1:]:
        gain = gain * one(*cut)
    return gain


def centred(stream_key, extent, scale, most, split=(), held_as=jnp.bfloat16):
    entries = jax.random.normal(stream_key, extent, jnp.float32) * scale
    if len(split) > 0:
        entries = steps_of(stream_key, extent, split, -0.22, 0.18) * entries
    return jnp.clip(entries, min=-most, max=most).astype(held_as)


def noise_with(own_key, shape, spread, limit, shards, heavy, kind=jnp.bfloat16):
    values = spread * jax.random.normal(own_key, shape, jnp.float32)
    if shards:
        values = values * steps_of(own_key, shape, shards, -0.22, 0.18)
    return jnp.clip(spiked(values, jax.random.fold_in(own_key, 3), *heavy), -limit, limit).astype(kind)


def setup_inputs(seed: int = 0) -> dict:
    key_list = jax.random.split(jax.random.key(seed), 4)
    inputs = noise_with(key_list[0], (MB, TOKENS, DIN), 1.0, 24.0, ((1, 128),), (1, 2, 128, 5.5))
    weight = centred(key_list[1], (DIN, DOUT), DIN ** -0.5, 0.078125, ((0, 16), (1, 8)))
    cotangent = centred(key_list[2], (MB, TOKENS, DOUT), 1.0, 6.0, ((1, 16), (2, 8)))
    return dict(inputs=inputs, weight=weight, cotangent=cotangent)


def reference(inputs, weight, cotangent):
    outputs = []
    in_grads = []
    width = DOUT // N_LOCAL
    for micro_step in range(MB):
        outputs.append(jnp.dot(inputs[micro_step], weight, preferred_element_type=jnp.float32).astype(jnp.bfloat16))
        total = jnp.zeros((TOKENS, DIN), jnp.float32)
        for block in range(N_LOCAL):
            cot_block = cotangent[micro_step][:, block * width:(block + 1) * width]
            w_block = weight[:, block * width:(block + 1) * width]
            part = jnp.dot(cot_block, w_block.T, preferred_element_type=jnp.float32).astype(jnp.bfloat16)
            total = total + part.astype(jnp.float32)
        in_grads.append(total.astype(jnp.bfloat16))
    group_size = TOKENS // N_NODE
    grad_scale = 1.0 / math.sqrt(MB * TOKENS)
    xs_group = jnp.transpose(inputs.reshape(MB, N_NODE, group_size, DIN), (1, 0, 2, 3))
    cs_group = jnp.transpose(cotangent.reshape(MB, N_NODE, group_size, DOUT), (1, 0, 2, 3))

    def add_group(total, pair):
        x_group, c_group = pair
        part = jnp.einsum('mtd,mte->de', x_group.astype(jnp.float32), c_group.astype(jnp.float32))
        part = (part * grad_scale).astype(jnp.bfloat16)
        return (total + part.astype(jnp.float32), None)
    grad_total, unused = lax.scan(add_group, jnp.zeros((DIN, DOUT), jnp.float32), (xs_group, cs_group))
    return (jnp.stack(outputs), jnp.stack(in_grads), grad_total.astype(jnp.bfloat16))
```

```python
import functools
import math

import jax
import jax.numpy as jnp
from jax import lax
from jax.experimental import pallas as pl
from jax.experimental.pallas import tpu as pltpu
from jax.sharding import PartitionSpec as P

MESH = pl.DeviceIdType.MESH
F32 = jnp.float32
BF16 = jnp.bfloat16
NX = 4
ROWS = 64
STRIPE = 384
BLOCK = 768
GROUP = 512
HALF = 3072
WIDE = 1536
UNIT = 768
TILE = 256


def kernel(
    scale, x_ref, w_ref, c_ref, y_out, dx_out, dw_out,
    xg, wg, cg, dxp, fx, nx, dxf, ysend, yrecv, yfin, dws, dwr, dwq, fy, ny, osnd, orcv, dwf,
    xloc, zx_s, zx_r, cloc, c_s, c_r, wloc, wd_s, wd_r, wo_s, wo_r, xr_s, xr_r, yr_s, yr_r, sib_s, sib_r,
    dx_s, dx_r, dxz_s, dxz_r, dxl, yy_s, yy_r, yl, dws_s, dws_r, dy_s, dy_r, do_s, do_r, dd_s, dd_r, ddl,
):
    node, local = lax.axis_index("node"), lax.axis_index("local")
    x, l = local // 2, local % 2
    y, h, c = node // 4, (node // 2) % 2, node % 2
    t = (l + h) % 2
    lw = (c + h) % 2
    keeps = c == t

    def dev(x_, y_, h_, l_, c_):
        return ((y_ * 2 + h_) * 2 + c_, x_ * 2 + l_)

    def up(v, by):
        return lax.rem(v + by + NX, NX)

    zp = dev(x, y, h, 1 - l, c)
    sib = dev(x, y, h, l, 1 - c)
    diag = dev(x, y, h, 1 - l, 1 - c)
    outer = dev(x, y, 1 - h, 1 - l, 1 - c)
    step = (1, -1)
    xn = [dev(up(x, s), y, h, l, c) for s in step]
    yn = [dev(x, up(y, s), h, l, c) for s in step]

    def remote(src, dst, ssem, rsem, to):
        return pltpu.make_async_remote_copy(
            src_ref=src, dst_ref=dst, send_sem=ssem, recv_sem=rsem, device_id=to, device_id_type=MESH
        )

    def at(start, size, multiple):
        return pl.ds(pl.multiple_of(start, multiple), size)

    lo = at(l * BLOCK, BLOCK, BLOCK)
    lz = at((1 - l) * BLOCK, BLOCK, BLOCK)
    lwc = at(lw * BLOCK, BLOCK, BLOCK)
    lwz = at((1 - lw) * BLOCK, BLOCK, BLOCK)

    def x_rows(x_, l_):
        return at(x_ * (2 * ROWS) + l_ * ROWS, ROWS, ROWS)

    def x_local(s):
        return pltpu.make_async_copy(
            x_ref.at[:, :, at((2 * s + t) * STRIPE, STRIPE, STRIPE)],
            xg.at[:, x_rows(x, l), s * STRIPE : (s + 1) * STRIPE],
            xloc.at[s],
        )

    def x_swap(s, l_from):
        return remote(
            x_ref.at[:, :, at((2 * s + 1 - t) * STRIPE, STRIPE, STRIPE)],
            xg.at[:, x_rows(x, l_from), s * STRIPE : (s + 1) * STRIPE],
            zx_s.at[s], zx_r.at[s], zp,
        )

    def x_ring(x_, lrel, d, k):
        micro = d if k != 1 else 1 - d
        owner = x_ if k < 2 else up(x_, -step[d])
        part = xg.at[micro, x_rows(owner, l if lrel == 0 else 1 - l)]
        return remote(part, part, xr_s.at[lrel, d, k], xr_r.at[lrel, d, k], xn[d])

    def stripe(y_, hrel):
        return y_ * 2 + (h if hrel == 0 else 1 - h)

    def w_part(s, cols, piece=None):
        if piece is None:
            return wg.at[at(s * STRIPE, STRIPE, STRIPE), cols]
        return wg.at[at(s * STRIPE + piece * (STRIPE // 2), STRIPE // 2, STRIPE // 2), cols]

    def w_local():
        return pltpu.make_async_copy(w_ref, w_part(stripe(y, 0), lwc), wloc)

    def w_diag(cols):
        return remote(w_ref, w_part(stripe(y, 0), cols), wd_s, wd_r, diag)

    def w_outer(hrel):
        part = w_part(stripe(y, hrel), lwc)
        return remote(part, part, wo_s, wo_r, outer)

    def w_ring(y_, hrel, d, k):
        piece = d if k != 1 else 1 - d
        owner = y_ if k < 2 else up(y_, -step[d])
        part = w_part(stripe(owner, hrel), lwc, piece)
        return remote(part, part, yr_s.at[hrel, d, k], yr_r.at[hrel, d, k], yn[d])

    def w_sib(s, cols):
        part = w_part(s, cols)
        return remote(part, part, sib_s.at[s], sib_r.at[s], sib)

    def c_local():
        return pltpu.make_async_copy(c_ref, cg.at[:, :, lo], cloc)

    def c_swap(cols):
        return remote(c_ref, cg.at[:, :, cols], c_s, c_r, zp)

    def unit_of(i):
        return up(y, i + jnp.where(i == 2, 1, 0) - jnp.where(i == 3, 1, 0))

    def unit_back(i):
        return up(y, jnp.where(i == 0, 2, jnp.where(i == 1, 1, jnp.where(i == 2, 3, 0))))

    def dx_ring(i, d, k):
        ks = at(unit_of(i) * UNIT, UNIT, UNIT)
        micro = d if k != 1 else 1 - d
        to = up(x, 2) if k == 0 else up(x, step[d])
        src = dxp.at[micro, at(to * (2 * ROWS), 2 * ROWS, 2 * ROWS), ks]
        dst = fx.at[d, :, ks] if k == 0 else nx.at[d, micro, :, ks]
        return remote(src, dst, dx_s.at[i, d, k], dx_r.at[i, d, k], xn[d])

    def dx_back(i, e, t_, mine):
        s = unit_of(i) * 2 + e
        rows = at((l if mine else 1 - l) * ROWS, ROWS, ROWS)
        src = dxf.at[:, rows, at(s * STRIPE, STRIPE, STRIPE)]
        dst = dx_out.at[:, :, at((2 * s + t_) * STRIPE, STRIPE, STRIPE)]
        if mine:
            return pltpu.make_async_copy(src, dst, dxl.at[i, e])
        return remote(src, dst, dxz_s.at[i, e], dxz_r.at[i, e], zp)

    def y_swap(m):
        return remote(ysend.at[m], yrecv.at[m], yy_s.at[m], yy_r.at[m], zp)

    def y_store(m):
        return pltpu.make_async_copy(yfin.at[m], y_out.at[m], yl.at[m])

    def dw_sib(i):
        rows = at(unit_back(i) * UNIT, UNIT, UNIT)
        return remote(dws.at[rows], dwr.at[rows], dws_s.at[i], dws_r.at[i], sib)

    def dw_rows(y_, piece):
        return at(y_ * UNIT + piece * STRIPE, STRIPE, STRIPE)

    def dw_ring(d, k):
        piece = d if k != 1 else 1 - d
        to = up(y, 2) if k == 0 else up(y, step[d])
        dst = fy.at[d] if k == 0 else ny.at[d, piece * STRIPE : (piece + 1) * STRIPE]
        return remote(dwq.at[dw_rows(to, piece)], dst, dy_s.at[d, k], dy_r.at[d, k], yn[d])

    def dw_outer():
        return remote(osnd, orcv, do_s, do_r, outer)

    def dw_diag():
        return remote(dwf, dw_out, dd_s, dd_r, diag)

    def dw_local():
        return pltpu.make_async_copy(dwf, dw_out, ddl)

    for s in range(8):
        x_local(s).start()
    c_local().start()

    @pl.when(keeps)
    def _():
        w_local().start()

    barrier = pltpu.get_barrier_semaphore()
    friends = [zp, sib, diag, outer, *xn, *yn]
    for friend in friends:
        pl.semaphore_signal(barrier, inc=1, device_id=friend, device_id_type=MESH)
    pl.semaphore_wait(barrier, len(friends))

    @pl.when(jnp.logical_not(keeps))
    def _():
        w_diag(lo).start()

    for s in range(8):
        x_swap(s, l).start()
    for s in range(8):
        x_local(s).wait()
    for k in (0, 1):
        for d in (0, 1):
            x_ring(x, 0, d, k).start()

    @pl.when(keeps)
    def _():
        w_local().wait()

    @pl.when(jnp.logical_not(keeps))
    def _():
        w_diag(lwc).wait_recv()

    w_outer(0).start()
    for k in (0, 1):
        for d in (0, 1):
            w_ring(y, 0, d, k).start()
    w_sib(stripe(y, 0), lwc).start()

    def x_from(d):
        return up(x, -step[d])

    def y_from(d):
        return up(y, -step[d])

    for d in (0, 1):
        x_ring(x_from(d), 0, d, 0).wait_recv()
        x_ring(x, 0, d, 2).start()
    for d in (0, 1):
        w_ring(y_from(d), 0, d, 0).wait_recv()
        w_ring(y, 0, d, 2).start()
    w_outer(1).wait_recv()
    for k in (0, 1):
        for d in (0, 1):
            w_ring(y, 1, d, k).start()
    w_sib(stripe(y, 1), lwc).start()
    for s in range(8):
        x_swap(s, l).wait_send()
    c_swap(lo).start()
    for s in range(8):
        x_swap(s, 1 - l).wait_recv()
    for k in (0, 1):
        for d in (0, 1):
            x_ring(x, 1, d, k).start()
    for d in (0, 1):
        w_ring(y_from(d), 0, d, 1).wait_recv()
        w_sib(stripe(y_from(d), 0), lwc).start()
    for d in (0, 1):
        w_ring(y_from(d), 0, d, 2).wait_recv()
    w_sib(stripe(up(y, 2), 0), lwc).start()
    for d in (0, 1):
        w_ring(y_from(d), 1, d, 0).wait_recv()
        w_ring(y, 1, d, 2).start()
    for d in (0, 1):
        x_ring(x_from(d), 1, d, 0).wait_recv()
        x_ring(x, 1, d, 2).start()
    for d in (0, 1):
        w_ring(y_from(d), 1, d, 1).wait_recv()
        w_sib(stripe(y_from(d), 1), lwc).start()
    for d in (0, 1):
        w_ring(y_from(d), 1, d, 2).wait_recv()
    w_sib(stripe(up(y, 2), 1), lwc).start()
    for d in (0, 1):
        x_ring(x_from(d), 0, d, 1).wait_recv()
        x_ring(x_from(d), 0, d, 2).wait_recv()
    for s in range(8):
        w_sib(s, lwz).wait_recv()
    for d in (0, 1):
        x_ring(x_from(d), 1, d, 1).wait_recv()
        x_ring(x_from(d), 1, d, 2).wait_recv()

    for m in (0, 1):

        @pl.loop(0, BLOCK // TILE)
        def _(j):
            cols = at((1 - l) * BLOCK + j * TILE, TILE, TILE)
            ysend[m, :, at(j * TILE, TILE, TILE)] = jnp.dot(
                xg[m], wg[:, cols], preferred_element_type=F32
            ).astype(BF16)

        y_swap(m).start()

    c_local().wait()
    c_swap(lz).wait_recv()

    def dx_relay(i):
        ks = at(unit_of(i) * UNIT, UNIT, UNIT)
        for d in (0, 1):
            dx_ring(i, d, 0).wait_recv()
            rows = at(up(x, step[d]) * (2 * ROWS), 2 * ROWS, 2 * ROWS)
            dxp[d, rows, ks] = (dxp[d, rows, ks].astype(F32) + fx[d, :, ks].astype(F32)).astype(BF16)
            dx_ring(i, d, 2).start()

    def dx_final(i):
        ks = at(unit_of(i) * UNIT, UNIT, UNIT)
        for d in (0, 1):
            for k in (1, 2):
                dx_ring(i, d, k).wait_recv()
        mine = at(x * (2 * ROWS), 2 * ROWS, 2 * ROWS)
        for m in (0, 1):
            dxf[m, :, ks] = (
                dxp[m, mine, ks].astype(F32) + nx[0, m, :, ks].astype(F32) + nx[1, m, :, ks].astype(F32)
            ).astype(BF16)
        for e in (0, 1):
            dx_back(i, e, t, False).start()
            dx_back(i, e, t, True).start()

    @pl.loop(0, 4)
    def _(i):
        base = unit_back(i) * UNIT

        @pl.loop(0, UNIT // TILE)
        def _(j):
            ks = at(base + j * TILE, TILE, TILE)
            xt = xg[:, :, ks].reshape(2 * GROUP, TILE).T
            for q, (off, dst) in enumerate((((1 - lw) * BLOCK, dws), (lw * BLOCK, dwq))):
                for n in range(BLOCK // TILE):
                    cv = cg[:, :, at(off + n * TILE, TILE, TILE)].reshape(2 * GROUP, TILE)
                    acc = jnp.dot(xt, cv, preferred_element_type=F32)
                    dst[ks, n * TILE : (n + 1) * TILE] = (acc * scale).astype(BF16)

        dw_sib(i).start()

        @pl.loop(0, UNIT // TILE)
        def _(j):
            ks = at(unit_of(i) * UNIT + j * TILE, TILE, TILE)
            acc = lax.dot_general(
                cg[...].reshape(2 * GROUP, WIDE), wg[ks, :], (((1,), (1,)), ((), ())),
                preferred_element_type=F32,
            )
            dxp[:, :, ks] = acc.astype(BF16).reshape(2, GROUP, TILE)

        for k in (0, 1):
            for d in (0, 1):
                dx_ring(i, d, k).start()

        dw_sib(i).wait_recv()

        @pl.loop(0, 4)
        def _(j):
            part = at(base + j * (UNIT // 4), UNIT // 4, UNIT // 4)
            dwq[part, :] = (dwq[part, :].astype(F32) + dwr[part, :].astype(F32)).astype(BF16)

        @pl.when(i == 0)
        def _():
            dw_ring(0, 0).start()
            dw_ring(1, 0).start()

        @pl.when(i == 1)
        def _():
            dw_ring(0, 1).start()

        @pl.when(i == 2)
        def _():
            dw_ring(1, 1).start()

        @pl.when(i > 0)
        def _():
            dx_relay(i - 1)

    for d in (0, 1):
        dw_ring(d, 0).wait_recv()
        rows = dw_rows(up(y, step[d]), d)
        dwq[rows, :] = (dwq[rows, :].astype(F32) + fy[d].astype(F32)).astype(BF16)
        dw_ring(d, 2).start()
    dx_relay(3)
    dx_final(0)

    for m in (0, 1):
        y_swap(m).wait_recv()

        @pl.loop(0, BLOCK // TILE)
        def _(j):
            cols = at(l * BLOCK + j * TILE, TILE, TILE)
            js = at(j * TILE, TILE, TILE)
            acc = jnp.dot(xg[m], wg[:, cols], preferred_element_type=F32)
            yfin[m, :, js] = (acc + yrecv[m, :, js].astype(F32)).astype(BF16)

        y_store(m).start()

    dx_final(1)
    for d in (0, 1):
        for k in (1, 2):
            dw_ring(d, k).wait_recv()

    def dw_total(h_):
        rows = at(h_ * STRIPE, STRIPE, STRIPE)
        return dwq[dw_rows(y, h_), :].astype(F32) + ny[0, rows, :].astype(F32) + ny[1, rows, :].astype(F32)

    osnd[...] = dw_total(1 - h).astype(BF16)
    dw_outer().start()
    dx_final(2)
    dx_final(3)
    dw_outer().wait_recv()
    dwf[...] = (dw_total(h) + orcv[...].astype(F32)).astype(BF16)

    @pl.when(keeps)
    def _():
        dw_local().start()
        dw_local().wait()

    @pl.when(jnp.logical_not(keeps))
    def _():
        dw_diag().start()
        dw_diag().wait()
        w_diag(lo).wait_send()

    for s in range(8):
        w_sib(s, lwc).wait_send()
    w_outer(0).wait_send()
    c_swap(lo).wait_send()
    for rel in (0, 1):
        for d in (0, 1):
            for k in range(3):
                x_ring(x, rel, d, k).wait_send()
                w_ring(y, rel, d, k).wait_send()
    for d in (0, 1):
        for k in range(3):
            dw_ring(d, k).wait_send()
    dw_outer().wait_send()
    for m in (0, 1):
        y_swap(m).wait_send()
        y_store(m).wait()

    @pl.loop(0, 4)
    def _(i):
        dw_sib(i).wait_send()
        for d in (0, 1):
            for k in range(3):
                dx_ring(i, d, k).wait_send()
        for e in (0, 1):
            dx_back(i, e, t, False).wait_send()
            dx_back(i, e, 1 - t, False).wait_recv()
            dx_back(i, e, t, True).wait()


def body(inputs, weight, cotangent):
    scale = 1.0 / math.sqrt(
        inputs.shape[0] * inputs.shape[1] * lax.axis_size("node") * lax.axis_size("local")
    )
    dma = pltpu.SemaphoreType.DMA
    vmem = [
        (2, GROUP, HALF), (HALF, WIDE), (2, GROUP, WIDE),
        (2, GROUP, HALF), (2, 2 * ROWS, HALF), (2, 2, 2 * ROWS, HALF), (2, 2 * ROWS, HALF),
        (2, GROUP, BLOCK), (2, GROUP, BLOCK), (2, GROUP, BLOCK),
        (HALF, BLOCK), (HALF, BLOCK), (HALF, BLOCK),
        (2, STRIPE, BLOCK), (2, UNIT, BLOCK), (STRIPE, BLOCK), (STRIPE, BLOCK), (STRIPE, BLOCK),
    ]
    sems = [
        (8,), (8,), (8,), (), (), (), (), (), (), (), (), (2, 2, 3), (2, 2, 3), (2, 2, 3), (2, 2, 3), (8,), (8,),
        (4, 2, 3), (4, 2, 3), (4, 2), (4, 2), (4, 2), (2,), (2,), (2,), (4,), (4,), (2, 3), (2, 3), (), (), (), (), (),
    ]
    out = [
        jax.ShapeDtypeStruct((2, GROUP, BLOCK), BF16),
        jax.ShapeDtypeStruct((2, ROWS, 2 * HALF), BF16),
        jax.ShapeDtypeStruct((STRIPE, BLOCK), BF16),
    ]
    return pl.pallas_call(
        functools.partial(kernel, scale),
        out_shape=out,
        in_specs=[pl.BlockSpec(memory_space=pl.ANY)] * 3,
        out_specs=[pl.BlockSpec(memory_space=pl.ANY)] * 3,
        scratch_shapes=[pltpu.VMEM(s, BF16) for s in vmem] + [dma(s) if s else dma for s in sems],
        compiler_params=pltpu.CompilerParams(
            collective_id=0, has_side_effects=True, vmem_limit_bytes=62 * 2**20
        ),
        cost_estimate=pl.CostEstimate(flops=29 * 10**9, bytes_accessed=8 * 2**20, transcendentals=0),
    )(inputs, weight, cotangent)


def solution(mesh):
    return jax.shard_map(
        body,
        mesh=mesh,
        in_specs=(P(None, ("node", "local"), None), P("node", "local"), P(None, "node", "local")),
        out_specs=(P(None, "node", "local"), P(None, ("node", "local"), None), P("node", "local")),
        check_vma=False,
    )
```

```python
import functools
import math

import jax
import jax.numpy as jnp
from jax import lax
from jax.experimental import pallas as pl
from jax.experimental.pallas import tpu as pltpu
from jax.sharding import PartitionSpec as P

MESH = pl.DeviceIdType.MESH
F32 = jnp.float32
BF16 = jnp.bfloat16
NX = 4
ROWS = 64
STRIPE = 384
BLOCK = 768
GROUP = 512
HALF = 3072
WIDE = 1536
UNIT = 768
TILE = 256
FAR, BEFORE, OWN, AFTER = range(4)


def kernel(
    scale, x_ref, w_ref, c_ref, y_out, dx_out, dw_out,
    xg, wg, cg, dxp, fx, nx, dxf, ysend, yrecv, yfin, dwp, dwr, fy, ny, osnd, orcv, dwf,
    xloc, zx_s, zx_r, cloc, c_s, c_r, wloc, wd_s, wd_r, wo_s, wo_r, xr_s, xr_r, yr_s, yr_r, sib_s, sib_r,
    dx_s, dx_r, dxz_s, dxz_r, dxl, yy_s, yy_r, yl, dws_s, dws_r, dy_s, dy_r, do_s, do_r, dd_s, dd_r, ddl,
):
    node, local = lax.axis_index("node"), lax.axis_index("local")
    x, l = local // 2, local % 2
    y, h, c = node // 4, (node // 2) % 2, node % 2
    t = (l + h) % 2
    lw = (c + h) % 2
    keeps = c == t
    mine = jnp.where(keeps, 0, 1)

    def dev(x_, y_, h_, l_, c_):
        return ((y_ * 2 + h_) * 2 + c_, x_ * 2 + l_)

    def turn(v, by):
        return lax.rem(v + by + NX, NX)

    zp = dev(x, y, h, 1 - l, c)
    sib = dev(x, y, h, l, 1 - c)
    diag = dev(x, y, h, 1 - l, 1 - c)
    outer = dev(x, y, 1 - h, 1 - l, 1 - c)
    step = (1, -1)
    xn = [dev(turn(x, s), y, h, l, c) for s in step]
    yn = [dev(x, turn(y, s), h, l, c) for s in step]

    def remote(src, dst, ssem, rsem, to):
        return pltpu.make_async_remote_copy(
            src_ref=src, dst_ref=dst, send_sem=ssem, recv_sem=rsem, device_id=to, device_id_type=MESH
        )

    def at(start, size):
        return pl.ds(pl.multiple_of(start, size), size)

    def half(q):
        return slice(q * STRIPE, (q + 1) * STRIPE)

    lo = at(l * BLOCK, BLOCK)
    lz = at((1 - l) * BLOCK, BLOCK)
    lwc = at(lw * BLOCK, BLOCK)
    lwz = at((1 - lw) * BLOCK, BLOCK)

    def before(d):
        return BEFORE if d == 0 else AFTER

    def ahead(d):
        return AFTER if d == 0 else BEFORE

    def piece(d, k):
        return d if k != 1 else 1 - d

    def own_rows(rel):
        return at((l if rel == 0 else 1 - l) * ROWS, ROWS)

    def columns(v, e):
        return slice(v * UNIT + e * STRIPE, v * UNIT + (e + 1) * STRIPE)

    def stripe_columns(v, e, t_):
        return at(((turn(y, v - OWN) * 2 + e) * 2 + t_) * STRIPE, STRIPE)

    def x_local(v, e):
        return pltpu.make_async_copy(
            x_ref.at[:, :, stripe_columns(v, e, t)], xg.at[:, OWN, own_rows(0), columns(v, e)], xloc.at[v, e]
        )

    def x_swap(v, e, rel):
        return remote(
            x_ref.at[:, :, stripe_columns(v, e, 1 - t)], xg.at[:, OWN, own_rows(rel), columns(v, e)],
            zx_s.at[v, e], zx_r.at[v, e], zp,
        )

    def x_ring(rel, d, k):
        src, dst = (OWN, before(d)) if k < 2 else (before(d), FAR)
        m = piece(d, k)
        return remote(
            xg.at[m, src, own_rows(rel)], xg.at[m, dst, own_rows(rel)],
            xr_s.at[rel, d, k], xr_r.at[rel, d, k], xn[d],
        )

    def e_of(rel):
        return h if rel == 0 else 1 - h

    def w_part(v, e, cols):
        return wg.at[at(v * UNIT + e * STRIPE, STRIPE), cols]

    def w_local():
        return pltpu.make_async_copy(w_ref, w_part(OWN, h, lwc), wloc)

    def w_diag(cols):
        return remote(w_ref, w_part(OWN, h, cols), wd_s, wd_r, diag)

    def w_outer(rel):
        part = w_part(OWN, e_of(rel), lwc)
        return remote(part, part, wo_s, wo_r, outer)

    def w_ring(rel, d, k):
        src, dst = (OWN, before(d)) if k < 2 else (before(d), FAR)
        src, dst = [
            wg.at[at(v * UNIT + e_of(rel) * STRIPE + piece(d, k) * (STRIPE // 2), STRIPE // 2), lwc] for v in (src, dst)
        ]
        return remote(src, dst, yr_s.at[rel, d, k], yr_r.at[rel, d, k], yn[d])

    def w_sib(v, rel, cols):
        part = w_part(v, e_of(rel), cols)
        return remote(part, part, sib_s.at[v, rel], sib_r.at[v, rel], sib)

    def c_rows(s):
        return c_ref.at[:, at(turn(x, s - OWN) * (2 * ROWS), 2 * ROWS)]

    def c_local(s):
        return pltpu.make_async_copy(c_rows(s), cg.at[:, s, :, lo], cloc.at[s])

    def c_swap(s, cols):
        return remote(c_rows(s), cg.at[:, s, :, cols], c_s.at[s], c_r.at[s], zp)

    def dx_ring(v, d, k):
        ks = at(v * UNIT, UNIT)
        m = piece(d, k)
        src = dxp.at[m, FAR if k == 0 else ahead(d), :, ks]
        dst = fx.at[d, :, ks] if k == 0 else nx.at[d, m, :, ks]
        return remote(src, dst, dx_s.at[v, d, k], dx_r.at[v, d, k], xn[d])

    def dx_back(v, e, t_, mine):
        src = dxf.at[:, own_rows(0 if mine else 1), at(v * UNIT + e * STRIPE, STRIPE)]
        dst = dx_out.at[:, :, stripe_columns(v, e, t_)]
        if mine:
            return pltpu.make_async_copy(src, dst, dxl.at[v, e])
        return remote(src, dst, dxz_s.at[v, e], dxz_r.at[v, e], zp)

    def y_swap(m):
        return remote(ysend.at[m], yrecv.at[m], yy_s.at[m], yy_r.at[m], zp)

    def y_store(m, s):
        return pltpu.make_async_copy(
            yfin.at[m, s], y_out.at[m, at(turn(x, s - OWN) * (2 * ROWS), 2 * ROWS)], yl.at[m, s]
        )

    def dw_sib(v):
        rows = at(v * UNIT, UNIT)
        return remote(dwp.at[1, rows], dwr.at[rows], dws_s.at[v], dws_r.at[v], sib)

    def dw_rows(v, e):
        return at(v * UNIT + e * STRIPE, STRIPE)

    def dw_ring(d, k, q):
        p = piece(d, k)
        src = dwp.at[0, dw_rows(FAR if k == 0 else ahead(d), p), half(q)]
        dst = fy.at[d, :, half(q)] if k == 0 else ny.at[d, half(p), half(q)]
        return remote(src, dst, dy_s.at[d, k, q], dy_r.at[d, k, q], yn[d])

    def dw_outer(q):
        return remote(osnd.at[:, half(q)], orcv.at[:, half(q)], do_s.at[q], do_r.at[q], outer)

    def dw_diag(q):
        return remote(dwf.at[:, half(q)], dw_out.at[:, half(q)], dd_s.at[q], dd_r.at[q], diag)

    def dw_local(q):
        return pltpu.make_async_copy(dwf.at[:, half(q)], dw_out.at[:, half(q)], ddl.at[q])

    def y_tile(m, off, j):
        cols = at(off * BLOCK + j * TILE, TILE)
        return jnp.dot(xg[m].reshape(GROUP, HALF), wg[:, cols], preferred_element_type=F32).reshape(4, 2 * ROWS, TILE)

    def dx_rows(v, slots):
        count = slots.stop - slots.start

        @pl.loop(0, UNIT // TILE)
        def _(j):
            ks = at(v * UNIT + j * TILE, TILE)
            acc = lax.dot_general(
                cg[:, slots].reshape(2 * count * 2 * ROWS, WIDE), wg[ks, :], (((1,), (1,)), ((), ())),
                preferred_element_type=F32,
            )
            dxp[:, slots, :, ks] = acc.astype(BF16).reshape(2, count, 2 * ROWS, TILE)

    def dx_far(v):
        dx_rows(v, slice(0, 1))

    def dx_near(v):
        dx_rows(v, slice(1, 4))
        for d in (0, 1):
            dx_ring(v, d, 1).start()

    def dx_relay(v):
        ks = at(v * UNIT, UNIT)
        for d in (0, 1):
            dx_ring(v, d, 0).wait_recv()
            dxp[d, ahead(d), :, ks] = (dxp[d, ahead(d), :, ks].astype(F32) + fx[d, :, ks].astype(F32)).astype(BF16)
            dx_ring(v, d, 2).start()

    def dx_final(v):
        ks = at(v * UNIT, UNIT)
        for k in (1, 2):
            for d in (0, 1):
                dx_ring(v, d, k).wait_recv()
        for m in (0, 1):
            dxf[m, :, ks] = (
                dxp[m, OWN, :, ks].astype(F32) + nx[0, m, :, ks].astype(F32) + nx[1, m, :, ks].astype(F32)
            ).astype(BF16)
        for e in (0, 1):
            dx_back(v, e, t, False).start()
            dx_back(v, e, t, True).start()

    def dw_block(v, own):
        off = (l if own else 1 - l) * BLOCK
        slot = mine if own else 1 - mine

        @pl.loop(0, UNIT // TILE)
        def _(j):
            ks = at(v * UNIT + j * TILE, TILE)
            xt = xg[:, :, :, ks].reshape(2 * GROUP, TILE).T
            for n in range(BLOCK // TILE):
                cv = cg[:, :, :, at(off + n * TILE, TILE)].reshape(2 * GROUP, TILE)
                acc = jnp.dot(xt, cv, preferred_element_type=F32)
                dwp[slot, ks, n * TILE : (n + 1) * TILE] = (acc * scale).astype(BF16)

        @pl.when(jnp.logical_not(keeps) if own else keeps)
        def _():
            dw_sib(v).start()

    def dw_merge(v):
        dw_sib(v).wait_recv()

        @pl.loop(0, 4)
        def _(j):
            part = at(v * UNIT + j * (UNIT // 4), UNIT // 4)
            dwp[0, part, :] = (dwp[0, part, :].astype(F32) + dwr[part, :].astype(F32)).astype(BF16)

    def dw_send_far():
        for q in (0, 1):
            for d in (0, 1):
                dw_ring(d, 0, q).start()

    def dw_send_near(d):
        for q in (0, 1):
            dw_ring(d, 1, q).start()

    def dw_relay(q):
        for d in (0, 1):
            dw_ring(d, 0, q).wait_recv()
            rows = dw_rows(ahead(d), d)
            dwp[0, rows, half(q)] = (dwp[0, rows, half(q)].astype(F32) + fy[d, :, half(q)].astype(F32)).astype(BF16)
            dw_ring(d, 2, q).start()

    def dw_total(e, q):
        rows = at(e * STRIPE, STRIPE)
        return (
            dwp[0, dw_rows(OWN, e), half(q)].astype(F32)
            + ny[0, rows, half(q)].astype(F32)
            + ny[1, rows, half(q)].astype(F32)
        )

    stripes = [(v, e) for v in range(4) for e in range(2)]
    both = (0, 1)
    for v, e in stripes:
        x_local(v, e).start()
    for s in range(4):
        c_local(s).start()

    @pl.when(keeps)
    def _():
        w_local().start()

    barrier = pltpu.get_barrier_semaphore()
    friends = [zp, sib, diag, outer, *xn, *yn]
    for friend in friends:
        pl.semaphore_signal(barrier, inc=1, device_id=friend, device_id_type=MESH)
    pl.semaphore_wait(barrier, len(friends))

    @pl.when(jnp.logical_not(keeps))
    def _():
        w_diag(lo).start()

    @pl.when(keeps)
    def _():
        for v, e in stripes:
            x_swap(v, e, 0).start()

    for v, e in stripes:
        x_local(v, e).wait()
    for k in both:
        for d in both:
            x_ring(0, d, k).start()

    @pl.when(keeps)
    def _():
        w_local().wait()

    @pl.when(jnp.logical_not(keeps))
    def _():
        w_diag(lo).wait_send()
        for v, e in stripes:
            x_swap(v, e, 0).start()
        w_diag(lwc).wait_recv()

    w_outer(0).start()
    for k in both:
        for d in both:
            w_ring(0, d, k).start()
    w_sib(OWN, 0, lwc).start()

    for d in both:
        x_ring(0, d, 0).wait_recv()
        x_ring(0, d, 2).start()
    for d in both:
        w_ring(0, d, 0).wait_recv()
        w_ring(0, d, 2).start()
    w_outer(1).wait_recv()
    for k in both:
        for d in both:
            w_ring(1, d, k).start()
    w_sib(OWN, 1, lwc).start()
    for v, e in stripes:
        x_swap(v, e, 0).wait_send()
    c_swap(FAR, lo).start()
    for v, e in stripes:
        x_swap(v, e, 1).wait_recv()
    for k in both:
        for d in both:
            x_ring(1, d, k).start()
    for d in both:
        w_ring(0, d, 1).wait_recv()
        w_sib(before(d), 0, lwc).start()
    for d in both:
        w_ring(0, d, 2).wait_recv()
    w_sib(FAR, 0, lwc).start()
    c_swap(FAR, lo).wait_send()
    for s in (AFTER, BEFORE, OWN):
        c_swap(s, lo).start()
    for d in both:
        w_ring(1, d, 0).wait_recv()
        w_ring(1, d, 2).start()
    for d in both:
        x_ring(1, d, 0).wait_recv()
        x_ring(1, d, 2).start()
    for d in both:
        w_ring(1, d, 1).wait_recv()
        w_sib(before(d), 1, lwc).start()

    def w_arrived(v):
        for rel in both:
            w_sib(v, rel, lwz).wait_recv()

    for s in (FAR, AFTER, BEFORE, OWN):
        c_local(s).wait()
    c_swap(FAR, lz).wait_recv()
    w_arrived(OWN)
    dx_far(OWN)
    for v in (AFTER, BEFORE):
        w_arrived(v)
        dx_far(v)
    for d in both:
        w_ring(1, d, 2).wait_recv()
    w_sib(FAR, 1, lwc).start()
    w_arrived(FAR)
    dx_far(FAR)
    for rel in both:
        for d in both:
            for k in (1, 2):
                x_ring(rel, d, k).wait_recv()
    for v in (OWN, AFTER, BEFORE, FAR):
        for d in both:
            dx_ring(v, d, 0).start()

    def y_first(m):
        @pl.loop(0, BLOCK // TILE)
        def _(j):
            ysend[m, :, :, at(j * TILE, TILE)] = y_tile(m, 1 - l, j).astype(BF16)

        y_swap(m).start()

    dw_block(FAR, True)
    y_first(0)
    dw_block(AFTER, True)

    @pl.when(keeps)
    def _():
        dw_merge(FAR)
        dw_send_far()

    dw_block(BEFORE, True)

    @pl.when(keeps)
    def _():
        dw_merge(AFTER)
        dw_send_near(0)

    y_first(1)

    @pl.when(keeps)
    def _():
        dw_merge(BEFORE)
        dw_send_near(1)

    dw_block(OWN, True)

    @pl.when(keeps)
    def _():
        dw_merge(OWN)

    for s in (AFTER, BEFORE, OWN):
        c_swap(s, lz).wait_recv()

    def pick(i, a, b, c_, d_):
        return jnp.where(i == 0, a, jnp.where(i == 1, b, jnp.where(i == 2, c_, d_)))

    def dx_order(i):
        return pick(i, OWN, AFTER, BEFORE, FAR)

    def dw_order(i):
        return pick(i, FAR, AFTER, BEFORE, OWN)

    @pl.loop(0, 4)
    def _(i):
        dw_block(dw_order(i), False)
        dx_near(dx_order(i))

        @pl.when(jnp.logical_not(keeps))
        def _():
            dw_merge(dw_order(i))

            @pl.when(i == 0)
            def _():
                dw_send_far()

            @pl.when(i == 1)
            def _():
                dw_send_near(0)

            @pl.when(i == 2)
            def _():
                dw_send_near(1)

        @pl.when(jnp.where(keeps, 0, 2) == i)
        def _():
            for q in both:
                dw_relay(q)

        dx_relay(dx_order(i))

    dx_final(OWN)
    for m in both:
        y_swap(m).wait_recv()

        @pl.loop(0, BLOCK // TILE)
        def _(j):
            js = at(j * TILE, TILE)
            yfin[m, :, :, js] = (y_tile(m, l, j) + yrecv[m, :, :, js].astype(F32)).astype(BF16)

        for s in range(4):
            y_store(m, s).start()

    dx_final(AFTER)
    for q in both:
        for d in both:
            for k in (1, 2):
                dw_ring(d, k, q).wait_recv()
        osnd[:, half(q)] = dw_total(1 - h, q).astype(BF16)
        dw_outer(q).start()
    dx_final(BEFORE)
    dx_final(FAR)
    for q in both:
        dw_outer(q).wait_recv()
        dwf[:, half(q)] = (dw_total(h, q) + orcv[:, half(q)].astype(F32)).astype(BF16)

        @pl.when(keeps)
        def _():
            dw_local(q).start()

        @pl.when(jnp.logical_not(keeps))
        def _():
            dw_diag(q).start()

    for q in both:

        @pl.when(keeps)
        def _():
            dw_local(q).wait()

        @pl.when(jnp.logical_not(keeps))
        def _():
            dw_diag(q).wait()

    for v in range(4):
        for rel in both:
            w_sib(v, rel, lwc).wait_send()
    w_outer(0).wait_send()
    for s in (AFTER, BEFORE, OWN):
        c_swap(s, lo).wait_send()
    for rel in both:
        for d in both:
            for k in range(3):
                x_ring(rel, d, k).wait_send()
                w_ring(rel, d, k).wait_send()
    for q in both:
        for d in both:
            for k in range(3):
                dw_ring(d, k, q).wait_send()
        dw_outer(q).wait_send()
    for m in both:
        y_swap(m).wait_send()
        for s in range(4):
            y_store(m, s).wait()

    @pl.loop(0, 4)
    def _(v):
        dw_sib(v).wait_send()
        for d in both:
            for k in range(3):
                dx_ring(v, d, k).wait_send()
        for e in both:
            dx_back(v, e, t, False).wait_send()
            dx_back(v, e, 1 - t, False).wait_recv()
            dx_back(v, e, t, True).wait()


def body(inputs, weight, cotangent):
    scale = 1.0 / math.sqrt(
        inputs.shape[0] * inputs.shape[1] * lax.axis_size("node") * lax.axis_size("local")
    )
    dma = pltpu.SemaphoreType.DMA
    vmem = [
        (2, 4, 2 * ROWS, HALF), (HALF, WIDE), (2, 4, 2 * ROWS, WIDE),
        (2, 4, 2 * ROWS, HALF), (2, 2 * ROWS, HALF), (2, 2, 2 * ROWS, HALF), (2, 2 * ROWS, HALF),
        (2, 4, 2 * ROWS, BLOCK), (2, 4, 2 * ROWS, BLOCK), (2, 4, 2 * ROWS, BLOCK),
        (2, HALF, BLOCK), (HALF, BLOCK),
        (2, STRIPE, BLOCK), (2, UNIT, BLOCK), (STRIPE, BLOCK), (STRIPE, BLOCK), (STRIPE, BLOCK),
    ]
    sems = [
        (4, 2), (4, 2), (4, 2), (4,), (4,), (4,), (), (), (), (), (), (2, 2, 3), (2, 2, 3), (2, 2, 3), (2, 2, 3), (4, 2), (4, 2),
        (4, 2, 3), (4, 2, 3), (4, 2), (4, 2), (4, 2), (2,), (2,), (2, 4), (4,), (4,), (2, 3, 2), (2, 3, 2), (2,), (2,),
        (2,), (2,), (2,),
    ]
    out = [
        jax.ShapeDtypeStruct((2, GROUP, BLOCK), BF16),
        jax.ShapeDtypeStruct((2, ROWS, 2 * HALF), BF16),
        jax.ShapeDtypeStruct((STRIPE, BLOCK), BF16),
    ]
    return pl.pallas_call(
        functools.partial(kernel, scale),
        out_shape=out,
        in_specs=[pl.BlockSpec(memory_space=pl.ANY)] * 3,
        out_specs=[pl.BlockSpec(memory_space=pl.ANY)] * 3,
        scratch_shapes=[pltpu.VMEM(s, BF16) for s in vmem] + [dma(s) if s else dma for s in sems],
        compiler_params=pltpu.CompilerParams(
            collective_id=0, has_side_effects=True, vmem_limit_bytes=62 * 2**20
        ),
        cost_estimate=pl.CostEstimate(flops=29 * 10**9, bytes_accessed=8 * 2**20, transcendentals=0),
    )(inputs, weight, cotangent)


def solution(mesh):
    return jax.shard_map(
        body,
        mesh=mesh,
        in_specs=(P(None, ("node", "local"), None), P("node", "local"), P(None, "node", "local")),
        out_specs=(P(None, "node", "local"), P(None, ("node", "local"), None), P("node", "local")),
        check_vma=False,
    )
```

```python
import functools
import math

import jax
import jax.numpy as jnp
from jax import lax
from jax.experimental import pallas as pl
from jax.experimental.pallas import tpu as pltpu
from jax.sharding import PartitionSpec as P

MESH = pl.DeviceIdType.MESH
F32 = jnp.float32
BF16 = jnp.bfloat16
NX = 4
ROWS = 64
STRIPE = 384
BLOCK = 768
GROUP = 512
HALF = 3072
WIDE = 1536
UNIT = 768
TILE = 256
FAR, BEFORE, OWN, AFTER = range(4)
FIRST = [(0, FAR), (1, FAR), (0, BEFORE), (1, AFTER)]
SECOND = [(1, BEFORE), (0, AFTER), (0, OWN), (1, OWN)]


def kernel(
    scale, x_ref, w_ref, c_ref, y_out, dx_out, dw_out,
    xg, wg, cg, dxp, fx, nx, dxf, ysend, yrecv, yfin, dwp, dwr, fy, ny, osnd, orcv, dwf,
    xloc, zx_s, zx_r, cloc, c_s, c_r, wloc, wd_s, wd_r, wo_s, wo_r, xr_s, xr_r, yr_s, yr_r, sib_s, sib_r,
    dx_s, dx_r, dxz_s, dxz_r, dxl, yy_s, yy_r, yl, dws_s, dws_r, dy_s, dy_r, do_s, do_r, dd_s, dd_r, ddl,
):
    node, local = lax.axis_index("node"), lax.axis_index("local")
    x, l = local // 2, local % 2
    y, h, c = node // 4, (node // 2) % 2, node % 2
    t = (l + h) % 2
    lw = (c + h) % 2
    keeps = c == t
    mine = jnp.where(keeps, 0, 1)

    def dev(x_, y_, h_, l_, c_):
        return ((y_ * 2 + h_) * 2 + c_, x_ * 2 + l_)

    def turn(v, by):
        return lax.rem(v + by + NX, NX)

    zp = dev(x, y, h, 1 - l, c)
    sib = dev(x, y, h, l, 1 - c)
    diag = dev(x, y, h, 1 - l, 1 - c)
    outer = dev(x, y, 1 - h, 1 - l, 1 - c)
    step = (1, -1)
    xn = [dev(turn(x, s), y, h, l, c) for s in step]
    yn = [dev(x, turn(y, s), h, l, c) for s in step]

    def remote(src, dst, ssem, rsem, to):
        return pltpu.make_async_remote_copy(
            src_ref=src, dst_ref=dst, send_sem=ssem, recv_sem=rsem, device_id=to, device_id_type=MESH
        )

    def at(start, size):
        return pl.ds(pl.multiple_of(start, size), size)

    def half(q):
        return slice(q * STRIPE, (q + 1) * STRIPE)

    lo = at(l * BLOCK, BLOCK)
    lz = at((1 - l) * BLOCK, BLOCK)
    lwc = at(lw * BLOCK, BLOCK)
    lwz = at((1 - lw) * BLOCK, BLOCK)

    def before(d):
        return BEFORE if d == 0 else AFTER

    def ahead(d):
        return AFTER if d == 0 else BEFORE

    def piece(d, k):
        return d if k != 1 else 1 - d

    def own_rows(rel):
        return at((l if rel == 0 else 1 - l) * ROWS, ROWS)

    def columns(v, e):
        return slice(v * UNIT + e * STRIPE, v * UNIT + (e + 1) * STRIPE)

    def stripe_columns(v, e, t_):
        return at(((turn(y, v - OWN) * 2 + e) * 2 + t_) * STRIPE, STRIPE)

    def x_local(v, e):
        return pltpu.make_async_copy(
            x_ref.at[:, :, stripe_columns(v, e, t)], xg.at[:, OWN, own_rows(0), columns(v, e)], xloc.at[v, e]
        )

    def x_swap(v, e, rel):
        return remote(
            x_ref.at[:, :, stripe_columns(v, e, 1 - t)], xg.at[:, OWN, own_rows(rel), columns(v, e)],
            zx_s.at[v, e], zx_r.at[v, e], zp,
        )

    def x_ring(rel, d, k):
        src, dst = (OWN, before(d)) if k < 2 else (before(d), FAR)
        m = piece(d, k)
        return remote(
            xg.at[m, src, own_rows(rel)], xg.at[m, dst, own_rows(rel)],
            xr_s.at[rel, d, k], xr_r.at[rel, d, k], xn[d],
        )

    def e_of(rel):
        return h if rel == 0 else 1 - h

    def w_part(v, e, cols):
        return wg.at[at(v * UNIT + e * STRIPE, STRIPE), cols]

    def w_local():
        return pltpu.make_async_copy(w_ref, w_part(OWN, h, lwc), wloc)

    def w_diag(cols):
        return remote(w_ref, w_part(OWN, h, cols), wd_s, wd_r, diag)

    def w_outer(rel):
        part = w_part(OWN, e_of(rel), lwc)
        return remote(part, part, wo_s, wo_r, outer)

    def w_ring(rel, d, k):
        src, dst = (OWN, before(d)) if k < 2 else (before(d), FAR)
        src, dst = [
            wg.at[at(v * UNIT + e_of(rel) * STRIPE + piece(d, k) * (STRIPE // 2), STRIPE // 2), lwc] for v in (src, dst)
        ]
        return remote(src, dst, yr_s.at[rel, d, k], yr_r.at[rel, d, k], yn[d])

    def w_sib(v, rel, cols):
        part = w_part(v, e_of(rel), cols)
        return remote(part, part, sib_s.at[v, rel], sib_r.at[v, rel], sib)

    def c_rows(m, s):
        return c_ref.at[m, at(turn(x, s - OWN) * (2 * ROWS), 2 * ROWS)]

    def c_local(m, s):
        return pltpu.make_async_copy(c_rows(m, s), cg.at[m, s, :, lo], cloc.at[m, s])

    def c_swap(m, s, cols):
        return remote(c_rows(m, s), cg.at[m, s, :, cols], c_s.at[m, s], c_r.at[m, s], zp)

    def dx_ring(v, d, k):
        ks = at(v * UNIT, UNIT)
        m = piece(d, k)
        src = dxp.at[m, FAR if k == 0 else ahead(d), :, ks]
        dst = fx.at[d, :, ks] if k == 0 else nx.at[d, m, :, ks]
        return remote(src, dst, dx_s.at[v, d, k], dx_r.at[v, d, k], xn[d])

    def dx_back(v, e, t_, mine):
        src = dxf.at[:, own_rows(0 if mine else 1), at(v * UNIT + e * STRIPE, STRIPE)]
        dst = dx_out.at[:, :, stripe_columns(v, e, t_)]
        if mine:
            return pltpu.make_async_copy(src, dst, dxl.at[v, e])
        return remote(src, dst, dxz_s.at[v, e], dxz_r.at[v, e], zp)

    def y_swap(m):
        return remote(ysend.at[m], yrecv.at[m], yy_s.at[m], yy_r.at[m], zp)

    def y_store(m, s):
        return pltpu.make_async_copy(
            yfin.at[m, s], y_out.at[m, at(turn(x, s - OWN) * (2 * ROWS), 2 * ROWS)], yl.at[m, s]
        )

    def dw_sib(v):
        rows = at(v * UNIT, UNIT)
        return remote(dwp.at[1, rows], dwr.at[rows], dws_s.at[v], dws_r.at[v], sib)

    def dw_rows(v, e):
        return at(v * UNIT + e * STRIPE, STRIPE)

    def dw_ring(d, k, q):
        p = piece(d, k)
        src = dwp.at[0, dw_rows(FAR if k == 0 else ahead(d), p), half(q)]
        dst = fy.at[d, :, half(q)] if k == 0 else ny.at[d, half(p), half(q)]
        return remote(src, dst, dy_s.at[d, k, q], dy_r.at[d, k, q], yn[d])

    def dw_outer(q):
        return remote(osnd.at[:, half(q)], orcv.at[:, half(q)], do_s.at[q], do_r.at[q], outer)

    def dw_diag(q):
        return remote(dwf.at[:, half(q)], dw_out.at[:, half(q)], dd_s.at[q], dd_r.at[q], diag)

    def dw_local(q):
        return pltpu.make_async_copy(dwf.at[:, half(q)], dw_out.at[:, half(q)], ddl.at[q])

    def y_tile(m, off, j):
        cols = at(off * BLOCK + j * TILE, TILE)
        return jnp.dot(xg[m].reshape(GROUP, HALF), wg[:, cols], preferred_element_type=F32).reshape(4, 2 * ROWS, TILE)

    def dx_rows(v, parts):
        @pl.loop(0, UNIT // TILE)
        def _(j):
            ks = at(v * UNIT + j * TILE, TILE)
            acc = lax.dot_general(
                jnp.concatenate([cg[m, s] for m, s in parts], axis=0), wg[ks, :], (((1,), (1,)), ((), ())),
                preferred_element_type=F32,
            )
            for i, (m, s) in enumerate(parts):
                dxp[m, s, :, ks] = acc[i * 2 * ROWS : (i + 1) * 2 * ROWS].astype(BF16)

    def dx_first(v):
        dx_rows(v, FIRST)
        for k in (0, 1):
            for d in (0, 1):
                dx_ring(v, d, k).start()

    def dx_relay(v):
        ks = at(v * UNIT, UNIT)
        for d in (0, 1):
            dx_ring(v, d, 0).wait_recv()
            dxp[d, ahead(d), :, ks] = (dxp[d, ahead(d), :, ks].astype(F32) + fx[d, :, ks].astype(F32)).astype(BF16)
            dx_ring(v, d, 2).start()

    def dx_final(v):
        ks = at(v * UNIT, UNIT)
        for k in (1, 2):
            for d in (0, 1):
                dx_ring(v, d, k).wait_recv()
        for m in (0, 1):
            dxf[m, :, ks] = (
                dxp[m, OWN, :, ks].astype(F32) + nx[0, m, :, ks].astype(F32) + nx[1, m, :, ks].astype(F32)
            ).astype(BF16)
        for e in (0, 1):
            dx_back(v, e, t, False).start()
            dx_back(v, e, t, True).start()

    def dw_block(v, own):
        off = (l if own else 1 - l) * BLOCK
        slot = mine if own else 1 - mine

        @pl.loop(0, UNIT // TILE)
        def _(j):
            ks = at(v * UNIT + j * TILE, TILE)
            xt = xg[:, :, :, ks].reshape(2 * GROUP, TILE).T
            for n in range(BLOCK // TILE):
                cv = cg[:, :, :, at(off + n * TILE, TILE)].reshape(2 * GROUP, TILE)
                acc = jnp.dot(xt, cv, preferred_element_type=F32)
                dwp[slot, ks, n * TILE : (n + 1) * TILE] = (acc * scale).astype(BF16)

        @pl.when(jnp.logical_not(keeps) if own else keeps)
        def _():
            dw_sib(v).start()

    def dw_merge(v):
        dw_sib(v).wait_recv()

        @pl.loop(0, 4)
        def _(j):
            part = at(v * UNIT + j * (UNIT // 4), UNIT // 4)
            dwp[0, part, :] = (dwp[0, part, :].astype(F32) + dwr[part, :].astype(F32)).astype(BF16)

    def dw_send_far():
        for q in (0, 1):
            for d in (0, 1):
                dw_ring(d, 0, q).start()

    def dw_send_near(d):
        for q in (0, 1):
            dw_ring(d, 1, q).start()

    def dw_relay(q):
        for d in (0, 1):
            dw_ring(d, 0, q).wait_recv()
            rows = dw_rows(ahead(d), d)
            dwp[0, rows, half(q)] = (dwp[0, rows, half(q)].astype(F32) + fy[d, :, half(q)].astype(F32)).astype(BF16)
            dw_ring(d, 2, q).start()

    def dw_total(e, q):
        rows = at(e * STRIPE, STRIPE)
        return (
            dwp[0, dw_rows(OWN, e), half(q)].astype(F32)
            + ny[0, rows, half(q)].astype(F32)
            + ny[1, rows, half(q)].astype(F32)
        )

    stripes = [(v, e) for v in range(4) for e in range(2)]
    both = (0, 1)
    for v, e in stripes:
        x_local(v, e).start()
    for m, s in FIRST + SECOND:
        c_local(m, s).start()

    @pl.when(keeps)
    def _():
        w_local().start()

    barrier = pltpu.get_barrier_semaphore()
    friends = [zp, sib, diag, outer, *xn, *yn]
    for friend in friends:
        pl.semaphore_signal(barrier, inc=1, device_id=friend, device_id_type=MESH)
    pl.semaphore_wait(barrier, len(friends))

    @pl.when(jnp.logical_not(keeps))
    def _():
        w_diag(lo).start()

    for v, e in stripes:
        x_swap(v, e, 0).start()

    def c_start():
        for m, s in FIRST + SECOND:
            c_swap(m, s, lo).start()

    pl.when(jnp.logical_not(keeps))(c_start)

    for v, e in stripes:
        x_local(v, e).wait()
    for k in both:
        for d in both:
            x_ring(0, d, k).start()

    @pl.when(keeps)
    def _():
        w_local().wait()

    @pl.when(jnp.logical_not(keeps))
    def _():
        w_diag(lo).wait_send()
        w_diag(lwc).wait_recv()

    w_outer(0).start()
    for k in both:
        for d in both:
            w_ring(0, d, k).start()
    w_sib(OWN, 0, lwc).start()

    for d in both:
        x_ring(0, d, 0).wait_recv()
        x_ring(0, d, 2).start()
    for d in both:
        w_ring(0, d, 0).wait_recv()
        w_ring(0, d, 2).start()
    w_outer(1).wait_recv()
    for k in both:
        for d in both:
            w_ring(1, d, k).start()
    w_sib(OWN, 1, lwc).start()
    for v, e in stripes:
        x_swap(v, e, 1).wait_recv()
    for k in both:
        for d in both:
            x_ring(1, d, k).start()
    pl.when(keeps)(c_start)
    for d in both:
        w_ring(0, d, 1).wait_recv()
        w_sib(before(d), 0, lwc).start()
    for d in both:
        w_ring(0, d, 2).wait_recv()
    w_sib(FAR, 0, lwc).start()
    for d in both:
        w_ring(1, d, 0).wait_recv()
        w_ring(1, d, 2).start()
    for d in both:
        x_ring(1, d, 0).wait_recv()
        x_ring(1, d, 2).start()
    for d in both:
        w_ring(1, d, 1).wait_recv()
        w_sib(before(d), 1, lwc).start()

    def w_arrived(v):
        for rel in both:
            w_sib(v, rel, lwz).wait_recv()

    for m, s in FIRST + SECOND:
        c_local(m, s).wait()
    for m, s in FIRST:
        c_swap(m, s, lz).wait_recv()
    w_arrived(OWN)
    w_arrived(AFTER)
    w_arrived(BEFORE)

    @pl.loop(0, 3)
    def _(i):
        dx_first(jnp.where(i == 0, OWN, jnp.where(i == 1, AFTER, BEFORE)))

    for d in both:
        w_ring(1, d, 2).wait_recv()
    w_sib(FAR, 1, lwc).start()
    w_arrived(FAR)
    dx_first(FAR)
    for rel in both:
        for d in both:
            for k in (1, 2):
                x_ring(rel, d, k).wait_recv()

    def y_first(m):
        @pl.loop(0, BLOCK // TILE)
        def _(j):
            ysend[m, :, :, at(j * TILE, TILE)] = y_tile(m, 1 - l, j).astype(BF16)

        y_swap(m).start()

    y_first(0)
    dw_block(FAR, True)
    dw_block(AFTER, True)

    @pl.when(keeps)
    def _():
        dw_merge(FAR)
        dw_send_far()

    dw_block(BEFORE, True)

    @pl.when(keeps)
    def _():
        dw_merge(AFTER)
        dw_send_near(0)

    y_first(1)

    @pl.when(keeps)
    def _():
        dw_merge(BEFORE)
        dw_send_near(1)

    dw_block(OWN, True)

    @pl.when(keeps)
    def _():
        dw_merge(OWN)

    for m, s in SECOND:
        c_swap(m, s, lz).wait_recv()
    sends = jnp.logical_not(keeps)

    @pl.loop(0, 3)
    def _(i):
        dw_block(jnp.where(i == 0, FAR, jnp.where(i == 1, AFTER, BEFORE)), False)

        @pl.when(keeps & (i == 0))
        def _():
            for q in both:
                dw_relay(q)

        @pl.when(sends & (i == 1))
        def _():
            dw_merge(FAR)
            dw_send_far()

        @pl.when(sends & (i == 2))
        def _():
            dw_merge(AFTER)
            dw_send_near(0)

    @pl.loop(0, 4)
    def _(i):
        v = jnp.where(i == 0, OWN, jnp.where(i == 1, AFTER, jnp.where(i == 2, BEFORE, FAR)))

        @pl.when(i == 3)
        def _():
            dw_block(OWN, False)

        dx_rows(v, SECOND)

        @pl.when(sends & (i == 0))
        def _():
            dw_merge(BEFORE)
            dw_send_near(1)

        dx_relay(v)

        @pl.when(sends & (i == 1))
        def _():
            for q in both:
                dw_relay(q)

        @pl.when(sends & (i == 3))
        def _():
            dw_merge(OWN)

    def y_second(m):
        y_swap(m).wait_recv()

        @pl.loop(0, BLOCK // TILE)
        def _(j):
            js = at(j * TILE, TILE)
            yfin[m, :, :, js] = (y_tile(m, l, j) + yrecv[m, :, :, js].astype(F32)).astype(BF16)

        for s in range(4):
            y_store(m, s).start()

    dx_final(OWN)
    dx_final(AFTER)
    for q in both:
        for d in both:
            for k in (1, 2):
                dw_ring(d, k, q).wait_recv()
        osnd[:, half(q)] = dw_total(1 - h, q).astype(BF16)
        dw_outer(q).start()
    y_second(0)
    dx_final(BEFORE)
    for q in both:
        dw_outer(q).wait_recv()
        dwf[:, half(q)] = (dw_total(h, q) + orcv[:, half(q)].astype(F32)).astype(BF16)

        @pl.when(keeps)
        def _():
            dw_local(q).start()

        @pl.when(jnp.logical_not(keeps))
        def _():
            dw_diag(q).start()

    y_second(1)
    dx_final(FAR)

    for q in both:

        @pl.when(keeps)
        def _():
            dw_local(q).wait()

        @pl.when(jnp.logical_not(keeps))
        def _():
            dw_diag(q).wait()

    for v in range(4):
        for rel in both:
            w_sib(v, rel, lwc).wait_send()
    w_outer(0).wait_send()
    for v, e in stripes:
        x_swap(v, e, 0).wait_send()
    for m, s in FIRST + SECOND:
        c_swap(m, s, lo).wait_send()
    for rel in both:
        for d in both:
            for k in range(3):
                x_ring(rel, d, k).wait_send()
                w_ring(rel, d, k).wait_send()
    for q in both:
        for d in both:
            for k in range(3):
                dw_ring(d, k, q).wait_send()
        dw_outer(q).wait_send()
    for m in both:
        y_swap(m).wait_send()
        for s in range(4):
            y_store(m, s).wait()

    @pl.loop(0, 4)
    def _(v):
        dw_sib(v).wait_send()
        for d in both:
            for k in range(3):
                dx_ring(v, d, k).wait_send()
        for e in both:
            dx_back(v, e, t, False).wait_send()
            dx_back(v, e, 1 - t, False).wait_recv()
            dx_back(v, e, t, True).wait()


def hand_on(y_ref, dx_ref, dw_ref, y_out, dx_out, dw_out, y_buf, dx_buf, dw_buf, sem_in, sem_out):
    pieces = []
    for m in range(2):
        for i in range(2):
            pieces.append((y_ref, y_buf, y_out, (m, pl.ds(i * GROUP // 2, GROUP // 2))))
        pieces.append((dx_ref, dx_buf, dx_out, (m,)))
    pieces.append((dw_ref, dw_buf, dw_out, (pl.ds(0, STRIPE),)))
    loads = [pltpu.make_async_copy(a.at[i], b.at[i], sem_in.at[k]) for k, (a, b, _, i) in enumerate(pieces)]
    stores = [pltpu.make_async_copy(b.at[i], o.at[i], sem_out.at[k]) for k, (_, b, o, i) in enumerate(pieces)]
    for load in loads:
        load.start()
    for load, store in zip(loads, stores):
        load.wait()
        store.start()
    for store in stores:
        store.wait()


def body(inputs, weight, cotangent):
    scale = 1.0 / math.sqrt(
        inputs.shape[0] * inputs.shape[1] * lax.axis_size("node") * lax.axis_size("local")
    )
    dma = pltpu.SemaphoreType.DMA
    vmem = [
        (2, 4, 2 * ROWS, HALF), (HALF, WIDE), (2, 4, 2 * ROWS, WIDE),
        (2, 4, 2 * ROWS, HALF), (2, 2 * ROWS, HALF), (2, 2, 2 * ROWS, HALF), (2, 2 * ROWS, HALF),
        (2, 4, 2 * ROWS, BLOCK), (2, 4, 2 * ROWS, BLOCK), (2, 4, 2 * ROWS, BLOCK),
        (2, HALF, BLOCK), (HALF, BLOCK),
        (2, STRIPE, BLOCK), (2, UNIT, BLOCK), (STRIPE, BLOCK), (STRIPE, BLOCK), (STRIPE, BLOCK),
    ]
    sems = [
        (4, 2), (4, 2), (4, 2), (2, 4), (2, 4), (2, 4), (), (), (), (), (), (2, 2, 3), (2, 2, 3), (2, 2, 3), (2, 2, 3), (4, 2), (4, 2),
        (4, 2, 3), (4, 2, 3), (4, 2), (4, 2), (4, 2), (2,), (2,), (2, 4), (4,), (4,), (2, 3, 2), (2, 3, 2), (2,), (2,),
        (2,), (2,), (2,),
    ]
    out = [
        jax.ShapeDtypeStruct((2, GROUP, BLOCK), BF16),
        jax.ShapeDtypeStruct((2, ROWS, 2 * HALF), BF16),
        jax.ShapeDtypeStruct((STRIPE, BLOCK), BF16),
    ]
    results = pl.pallas_call(
        functools.partial(kernel, scale),
        out_shape=out,
        in_specs=[pl.BlockSpec(memory_space=pl.ANY)] * 3,
        out_specs=[pl.BlockSpec(memory_space=pl.ANY)] * 3,
        scratch_shapes=[pltpu.VMEM(s, BF16) for s in vmem] + [dma(s) if s else dma for s in sems],
        compiler_params=pltpu.CompilerParams(
            collective_id=0, has_side_effects=True, vmem_limit_bytes=62 * 2**20
        ),
        cost_estimate=pl.CostEstimate(flops=29 * 10**9, bytes_accessed=8 * 2**20, transcendentals=0),
    )(inputs, weight, cotangent)
    return pl.pallas_call(
        hand_on,
        out_shape=out,
        in_specs=[pl.BlockSpec(memory_space=pl.ANY)] * 3,
        out_specs=[pl.BlockSpec(memory_space=pl.ANY)] * 3,
        scratch_shapes=[pltpu.VMEM(o.shape, BF16) for o in out] + [dma((7,)), dma((7,))],
        compiler_params=pltpu.CompilerParams(vmem_limit_bytes=62 * 2**20),
    )(*results)


def solution(mesh):
    return jax.shard_map(
        body,
        mesh=mesh,
        in_specs=(P(None, ("node", "local"), None), P("node", "local"), P(None, "node", "local")),
        out_specs=(P(None, "node", "local"), P(None, ("node", "local"), None), P("node", "local")),
        check_vma=False,
    )
```

```python
import functools
import math

import jax
import jax.numpy as jnp
from jax import lax
from jax.experimental import pallas as pl
from jax.experimental.pallas import tpu as pltpu
from jax.sharding import PartitionSpec as P

MESH = pl.DeviceIdType.MESH
F32 = jnp.float32
BF16 = jnp.bfloat16
NX = 4
ROWS = 64
STRIPE = 384
BLOCK = 768
GROUP = 512
HALF = 3072
WIDE = 1536
UNIT = 768
TILE = 256
FAR, BEFORE, OWN, AFTER = range(4)
FIRST = [(0, FAR), (1, FAR), (0, BEFORE), (1, AFTER)]
SECOND = [(1, BEFORE), (0, AFTER), (0, OWN), (1, OWN)]


def kernel(
    scale, x_ref, w_ref, c_ref, y_out, dx_out, dw_out,
    xg, wg, cg, dxp, fx, nx, dxf, ysend, yrecv, yfin, dwp, dwr, fy, ny, osnd, orcv, dwf,
    xloc, zx_s, zx_r, cloc, c_s, c_r, wloc, wd_s, wd_r, wo_s, wo_r, xr_s, xr_r, yr_s, yr_r, sib_s, sib_r,
    dx_s, dx_r, dxz_s, dxz_r, dxl, yy_s, yy_r, yl, dws_s, dws_r, dy_s, dy_r, do_s, do_r, dd_s, dd_r, ddl,
):
    node, local = lax.axis_index("node"), lax.axis_index("local")
    x, l = local // 2, local % 2
    y, h, c = node // 4, (node // 2) % 2, node % 2
    t = (l + h) % 2
    lw = (c + h) % 2
    keeps = c == t
    mine = jnp.where(keeps, 0, 1)

    def dev(x_, y_, h_, l_, c_):
        return ((y_ * 2 + h_) * 2 + c_, x_ * 2 + l_)

    def turn(v, by):
        return lax.rem(v + by + NX, NX)

    zp = dev(x, y, h, 1 - l, c)
    sib = dev(x, y, h, l, 1 - c)
    diag = dev(x, y, h, 1 - l, 1 - c)
    outer = dev(x, y, 1 - h, 1 - l, 1 - c)
    step = (1, -1)
    xn = [dev(turn(x, s), y, h, l, c) for s in step]
    yn = [dev(x, turn(y, s), h, l, c) for s in step]

    def remote(src, dst, ssem, rsem, to):
        return pltpu.make_async_remote_copy(
            src_ref=src, dst_ref=dst, send_sem=ssem, recv_sem=rsem, device_id=to, device_id_type=MESH
        )

    def at(start, size):
        return pl.ds(pl.multiple_of(start, size), size)

    def third(q):
        return slice(q * TILE, (q + 1) * TILE)

    def half(q):
        return slice(q * STRIPE, (q + 1) * STRIPE)

    lo = at(l * BLOCK, BLOCK)
    lz = at((1 - l) * BLOCK, BLOCK)
    lwc = at(lw * BLOCK, BLOCK)
    lwz = at((1 - lw) * BLOCK, BLOCK)

    def before(d):
        return BEFORE if d == 0 else AFTER

    def ahead(d):
        return AFTER if d == 0 else BEFORE

    def piece(d, k):
        return d if k != 1 else 1 - d

    def own_rows(rel):
        return at((l if rel == 0 else 1 - l) * ROWS, ROWS)

    def columns(v, e):
        return slice(v * UNIT + e * STRIPE, v * UNIT + (e + 1) * STRIPE)

    def stripe_columns(v, e, t_):
        return at(((turn(y, v - OWN) * 2 + e) * 2 + t_) * STRIPE, STRIPE)

    def x_local(v, e):
        return pltpu.make_async_copy(
            x_ref.at[:, :, stripe_columns(v, e, t)], xg.at[:, OWN, own_rows(0), columns(v, e)], xloc.at[v, e]
        )

    def x_swap(v, e, rel):
        return remote(
            x_ref.at[:, :, stripe_columns(v, e, 1 - t)], xg.at[:, OWN, own_rows(rel), columns(v, e)],
            zx_s.at[v, e], zx_r.at[v, e], zp,
        )

    def x_ring(rel, d, k):
        src, dst = (OWN, before(d)) if k < 2 else (before(d), FAR)
        m = piece(d, k)
        return remote(
            xg.at[m, src, own_rows(rel)], xg.at[m, dst, own_rows(rel)],
            xr_s.at[rel, d, k], xr_r.at[rel, d, k], xn[d],
        )

    def e_of(rel):
        return h if rel == 0 else 1 - h

    def w_part(v, e, cols):
        return wg.at[at(v * UNIT + e * STRIPE, STRIPE), cols]

    def w_local():
        return pltpu.make_async_copy(w_ref, w_part(OWN, h, lwc), wloc)

    def w_diag(cols):
        return remote(w_ref, w_part(OWN, h, cols), wd_s, wd_r, diag)

    def w_outer(rel):
        part = w_part(OWN, e_of(rel), lwc)
        return remote(part, part, wo_s, wo_r, outer)

    def w_ring(rel, d, k):
        src, dst = (OWN, before(d)) if k < 2 else (before(d), FAR)
        src, dst = [
            wg.at[at(v * UNIT + e_of(rel) * STRIPE + piece(d, k) * (STRIPE // 2), STRIPE // 2), lwc] for v in (src, dst)
        ]
        return remote(src, dst, yr_s.at[rel, d, k], yr_r.at[rel, d, k], yn[d])

    def w_sib(v, rel, cols):
        part = w_part(v, e_of(rel), cols)
        return remote(part, part, sib_s.at[v, rel], sib_r.at[v, rel], sib)

    def c_rows(m, s):
        return c_ref.at[m, at(turn(x, s - OWN) * (2 * ROWS), 2 * ROWS)]

    def c_local(m, s):
        return pltpu.make_async_copy(c_rows(m, s), cg.at[m, s, :, lo], cloc.at[m, s])

    def c_swap(m, s, cols):
        return remote(c_rows(m, s), cg.at[m, s, :, cols], c_s.at[m, s], c_r.at[m, s], zp)

    def dx_ring(v, d, k):
        ks = at(v * UNIT, UNIT)
        m = piece(d, k)
        src = dxp.at[m, FAR if k == 0 else ahead(d), :, ks]
        dst = fx.at[d, :, ks] if k == 0 else nx.at[d, m, :, ks]
        return remote(src, dst, dx_s.at[v, d, k], dx_r.at[v, d, k], xn[d])

    def dx_back(v, e, t_, mine):
        src = dxf.at[:, own_rows(0 if mine else 1), at(v * UNIT + e * STRIPE, STRIPE)]
        dst = dx_out.at[:, :, stripe_columns(v, e, t_)]
        if mine:
            return pltpu.make_async_copy(src, dst, dxl.at[v, e])
        return remote(src, dst, dxz_s.at[v, e], dxz_r.at[v, e], zp)

    def y_swap(m):
        return remote(ysend.at[m], yrecv.at[m], yy_s.at[m], yy_r.at[m], zp)

    def y_store(m, s):
        return pltpu.make_async_copy(
            yfin.at[m, s], y_out.at[m, at(turn(x, s - OWN) * (2 * ROWS), 2 * ROWS)], yl.at[m, s]
        )

    def dw_sib(v):
        rows = at(v * UNIT, UNIT)
        return remote(dwp.at[1, rows], dwr.at[rows], dws_s.at[v], dws_r.at[v], sib)

    def dw_rows(v, e):
        return at(v * UNIT + e * STRIPE, STRIPE)

    def dw_ring(d, k, q):
        p = piece(d, k)
        src = dwp.at[0, dw_rows(FAR if k == 0 else ahead(d), p), third(q)]
        dst = fy.at[d, :, third(q)] if k == 0 else ny.at[d, half(p), third(q)]
        return remote(src, dst, dy_s.at[d, k, q], dy_r.at[d, k, q], yn[d])

    def dw_outer(q):
        return remote(osnd.at[:, third(q)], orcv.at[:, third(q)], do_s.at[q], do_r.at[q], outer)

    def dw_diag(q):
        return remote(dwf.at[:, third(q)], dw_out.at[:, third(q)], dd_s.at[q], dd_r.at[q], diag)

    def dw_local(q):
        return pltpu.make_async_copy(dwf.at[:, third(q)], dw_out.at[:, third(q)], ddl.at[q])

    def y_tile(m, off, j):
        cols = at(off * BLOCK + j * TILE, TILE)
        return jnp.dot(xg[m].reshape(GROUP, HALF), wg[:, cols], preferred_element_type=F32).reshape(4, 2 * ROWS, TILE)

    def dx_rows(v, parts):
        @pl.loop(0, UNIT // TILE)
        def _(j):
            ks = at(v * UNIT + j * TILE, TILE)
            acc = lax.dot_general(
                jnp.concatenate([cg[m, s] for m, s in parts], axis=0), wg[ks, :], (((1,), (1,)), ((), ())),
                preferred_element_type=F32,
            )
            for i, (m, s) in enumerate(parts):
                dxp[m, s, :, ks] = acc[i * 2 * ROWS : (i + 1) * 2 * ROWS].astype(BF16)

    def dx_first(v):
        dx_rows(v, FIRST)
        for k in (0, 1):
            for d in (0, 1):
                dx_ring(v, d, k).start()

    def dx_relay(v):
        ks = at(v * UNIT, UNIT)
        for d in (0, 1):
            dx_ring(v, d, 0).wait_recv()
            dxp[d, ahead(d), :, ks] = (dxp[d, ahead(d), :, ks].astype(F32) + fx[d, :, ks].astype(F32)).astype(BF16)
            dx_ring(v, d, 2).start()

    def dx_final(v):
        ks = at(v * UNIT, UNIT)
        for k in (1, 2):
            for d in (0, 1):
                dx_ring(v, d, k).wait_recv()
        for m in (0, 1):
            dxf[m, :, ks] = (
                dxp[m, OWN, :, ks].astype(F32) + nx[0, m, :, ks].astype(F32) + nx[1, m, :, ks].astype(F32)
            ).astype(BF16)
        for e in (0, 1):
            dx_back(v, e, t, False).start()
            dx_back(v, e, t, True).start()

    def dw_block(v, own):
        off = (l if own else 1 - l) * BLOCK
        slot = mine if own else 1 - mine

        @pl.loop(0, UNIT // TILE)
        def _(j):
            ks = at(v * UNIT + j * TILE, TILE)
            xt = xg[:, :, :, ks].reshape(2 * GROUP, TILE).T
            for n in range(BLOCK // TILE):
                cv = cg[:, :, :, at(off + n * TILE, TILE)].reshape(2 * GROUP, TILE)
                acc = jnp.dot(xt, cv, preferred_element_type=F32)
                dwp[slot, ks, n * TILE : (n + 1) * TILE] = (acc * scale).astype(BF16)

        @pl.when(jnp.logical_not(keeps) if own else keeps)
        def _():
            dw_sib(v).start()

    def dw_merge(v):
        dw_sib(v).wait_recv()

        @pl.loop(0, 4)
        def _(j):
            part = at(v * UNIT + j * (UNIT // 4), UNIT // 4)
            dwp[0, part, :] = (dwp[0, part, :].astype(F32) + dwr[part, :].astype(F32)).astype(BF16)

    def dw_send_far():
        for q in range(3):
            for d in (0, 1):
                dw_ring(d, 0, q).start()

    def dw_send_near(d):
        for q in range(3):
            dw_ring(d, 1, q).start()

    def dw_relay(q):
        for d in (0, 1):
            dw_ring(d, 0, q).wait_recv()
            rows = dw_rows(ahead(d), d)
            dwp[0, rows, third(q)] = (dwp[0, rows, third(q)].astype(F32) + fy[d, :, third(q)].astype(F32)).astype(BF16)
            dw_ring(d, 2, q).start()

    def dw_total(e, q):
        rows = at(e * STRIPE, STRIPE)
        return (
            dwp[0, dw_rows(OWN, e), third(q)].astype(F32)
            + ny[0, rows, third(q)].astype(F32)
            + ny[1, rows, third(q)].astype(F32)
        )

    stripes = [(v, e) for v in range(4) for e in range(2)]
    both = (0, 1)
    for v, e in stripes:
        x_local(v, e).start()
    for m, s in FIRST + SECOND:
        c_local(m, s).start()

    @pl.when(keeps)
    def _():
        w_local().start()

    barrier = pltpu.get_barrier_semaphore()
    friends = [zp, sib, diag, outer, *xn, *yn]
    for friend in friends:
        pl.semaphore_signal(barrier, inc=1, device_id=friend, device_id_type=MESH)
    pl.semaphore_wait(barrier, len(friends))

    @pl.when(jnp.logical_not(keeps))
    def _():
        w_diag(lo).start()

    for v, e in stripes:
        x_swap(v, e, 0).start()

    def c_start():
        for m, s in FIRST + SECOND:
            c_swap(m, s, lo).start()

    pl.when(jnp.logical_not(keeps))(c_start)

    for v, e in stripes:
        x_local(v, e).wait()
    for k in both:
        for d in both:
            x_ring(0, d, k).start()

    @pl.when(keeps)
    def _():
        w_local().wait()

    @pl.when(jnp.logical_not(keeps))
    def _():
        w_diag(lo).wait_send()
        w_diag(lwc).wait_recv()

    w_outer(0).start()
    for k in both:
        for d in both:
            w_ring(0, d, k).start()
    w_sib(OWN, 0, lwc).start()

    for d in both:
        x_ring(0, d, 0).wait_recv()
        x_ring(0, d, 2).start()
    for d in both:
        w_ring(0, d, 0).wait_recv()
        w_ring(0, d, 2).start()
    w_outer(1).wait_recv()
    for k in both:
        for d in both:
            w_ring(1, d, k).start()
    w_sib(OWN, 1, lwc).start()
    for v, e in stripes:
        x_swap(v, e, 1).wait_recv()
    for k in both:
        for d in both:
            x_ring(1, d, k).start()
    pl.when(keeps)(c_start)
    for d in both:
        w_ring(0, d, 1).wait_recv()
        w_sib(before(d), 0, lwc).start()
    for d in both:
        w_ring(0, d, 2).wait_recv()
    w_sib(FAR, 0, lwc).start()
    for d in both:
        w_ring(1, d, 0).wait_recv()
        w_ring(1, d, 2).start()
    for d in both:
        x_ring(1, d, 0).wait_recv()
        x_ring(1, d, 2).start()
    for d in both:
        w_ring(1, d, 1).wait_recv()
        w_sib(before(d), 1, lwc).start()

    def w_arrived(v):
        for rel in both:
            w_sib(v, rel, lwz).wait_recv()

    for m, s in FIRST + SECOND:
        c_local(m, s).wait()
    for m, s in FIRST:
        c_swap(m, s, lz).wait_recv()
    w_arrived(OWN)
    w_arrived(AFTER)
    w_arrived(BEFORE)

    @pl.loop(0, 3)
    def _(i):
        dx_first(jnp.where(i == 0, OWN, jnp.where(i == 1, AFTER, BEFORE)))

    for d in both:
        w_ring(1, d, 2).wait_recv()
    w_sib(FAR, 1, lwc).start()
    w_arrived(FAR)
    dx_first(FAR)
    for rel in both:
        for d in both:
            for k in (1, 2):
                x_ring(rel, d, k).wait_recv()

    def y_first(m):
        @pl.loop(0, BLOCK // TILE)
        def _(j):
            ysend[m, :, :, at(j * TILE, TILE)] = y_tile(m, 1 - l, j).astype(BF16)

        y_swap(m).start()

    y_first(0)
    dw_block(FAR, True)
    dw_block(AFTER, True)

    @pl.when(keeps)
    def _():
        dw_merge(FAR)
        dw_send_far()

    dw_block(BEFORE, True)

    @pl.when(keeps)
    def _():
        dw_merge(AFTER)
        dw_send_near(0)

    y_first(1)

    @pl.when(keeps)
    def _():
        dw_merge(BEFORE)
        dw_send_near(1)

    dw_block(OWN, True)

    @pl.when(keeps)
    def _():
        dw_merge(OWN)

    for m, s in SECOND:
        c_swap(m, s, lz).wait_recv()
    sends = jnp.logical_not(keeps)

    @pl.loop(0, 3)
    def _(i):
        dw_block(jnp.where(i == 0, FAR, jnp.where(i == 1, AFTER, BEFORE)), False)

        @pl.when(keeps & (i == 0))
        def _():
            for q in range(3):
                dw_relay(q)

        @pl.when(sends & (i == 1))
        def _():
            dw_merge(FAR)
            dw_send_far()

        @pl.when(sends & (i == 2))
        def _():
            dw_merge(AFTER)
            dw_send_near(0)

    @pl.loop(0, 4)
    def _(i):
        v = jnp.where(i == 0, OWN, jnp.where(i == 1, AFTER, jnp.where(i == 2, BEFORE, FAR)))

        @pl.when(i == 3)
        def _():
            dw_block(OWN, False)

        dx_rows(v, SECOND)

        @pl.when(sends & (i == 0))
        def _():
            dw_merge(BEFORE)
            dw_send_near(1)

        dx_relay(v)

        @pl.when(sends & (i == 1))
        def _():
            for q in range(3):
                dw_relay(q)

        @pl.when(sends & (i == 3))
        def _():
            dw_merge(OWN)

    def y_second(m):
        y_swap(m).wait_recv()

        @pl.loop(0, BLOCK // TILE)
        def _(j):
            js = at(j * TILE, TILE)
            yfin[m, :, :, js] = (y_tile(m, l, j) + yrecv[m, :, :, js].astype(F32)).astype(BF16)

        for s in range(4):
            y_store(m, s).start()

    dx_final(OWN)
    dx_final(AFTER)
    for q in range(3):
        for d in both:
            for k in (1, 2):
                dw_ring(d, k, q).wait_recv()
        osnd[:, third(q)] = dw_total(1 - h, q).astype(BF16)
        dw_outer(q).start()
    dx_final(BEFORE)
    y_second(0)
    dx_final(FAR)
    for q in range(3):
        dw_outer(q).wait_recv()
        dwf[:, third(q)] = (dw_total(h, q) + orcv[:, third(q)].astype(F32)).astype(BF16)

        @pl.when(keeps)
        def _():
            dw_local(q).start()

        @pl.when(jnp.logical_not(keeps))
        def _():
            dw_diag(q).start()

    y_second(1)

    for q in range(3):

        @pl.when(keeps)
        def _():
            dw_local(q).wait()

        @pl.when(jnp.logical_not(keeps))
        def _():
            dw_diag(q).wait()

    for v in range(4):
        for rel in both:
            w_sib(v, rel, lwc).wait_send()
    w_outer(0).wait_send()
    for v, e in stripes:
        x_swap(v, e, 0).wait_send()
    for m, s in FIRST + SECOND:
        c_swap(m, s, lo).wait_send()
    for rel in both:
        for d in both:
            for k in range(3):
                x_ring(rel, d, k).wait_send()
                w_ring(rel, d, k).wait_send()
    for q in range(3):
        for d in both:
            for k in range(3):
                dw_ring(d, k, q).wait_send()
        dw_outer(q).wait_send()
    for m in both:
        y_swap(m).wait_send()
        for s in range(4):
            y_store(m, s).wait()

    @pl.loop(0, 4)
    def _(v):
        dw_sib(v).wait_send()
        for d in both:
            for k in range(3):
                dx_ring(v, d, k).wait_send()
        for e in both:
            dx_back(v, e, t, False).wait_send()
            dx_back(v, e, 1 - t, False).wait_recv()
            dx_back(v, e, t, True).wait()


def hand_on(y_ref, dx_ref, dw_ref, y_out, dx_out, dw_out, y_buf, dx_buf, dw_buf, sem_in, sem_out):
    pieces = []
    for m in range(2):
        for i in range(2):
            pieces.append((y_ref, y_buf, y_out, (m, pl.ds(i * GROUP // 2, GROUP // 2))))
        pieces.append((dx_ref, dx_buf, dx_out, (m,)))
    pieces.append((dw_ref, dw_buf, dw_out, (pl.ds(0, STRIPE),)))
    loads = [pltpu.make_async_copy(a.at[i], b.at[i], sem_in.at[k]) for k, (a, b, _, i) in enumerate(pieces)]
    stores = [pltpu.make_async_copy(b.at[i], o.at[i], sem_out.at[k]) for k, (_, b, o, i) in enumerate(pieces)]
    for load in loads:
        load.start()
    for load, store in zip(loads, stores):
        load.wait()
        store.start()
    for store in stores:
        store.wait()


def body(inputs, weight, cotangent):
    scale = 1.0 / math.sqrt(
        inputs.shape[0] * inputs.shape[1] * lax.axis_size("node") * lax.axis_size("local")
    )
    dma = pltpu.SemaphoreType.DMA
    vmem = [
        (2, 4, 2 * ROWS, HALF), (HALF, WIDE), (2, 4, 2 * ROWS, WIDE),
        (2, 4, 2 * ROWS, HALF), (2, 2 * ROWS, HALF), (2, 2, 2 * ROWS, HALF), (2, 2 * ROWS, HALF),
        (2, 4, 2 * ROWS, BLOCK), (2, 4, 2 * ROWS, BLOCK), (2, 4, 2 * ROWS, BLOCK),
        (2, HALF, BLOCK), (HALF, BLOCK),
        (2, STRIPE, BLOCK), (2, UNIT, BLOCK), (STRIPE, BLOCK), (STRIPE, BLOCK), (STRIPE, BLOCK),
    ]
    sems = [
        (4, 2), (4, 2), (4, 2), (2, 4), (2, 4), (2, 4), (), (), (), (), (), (2, 2, 3), (2, 2, 3), (2, 2, 3), (2, 2, 3), (4, 2), (4, 2),
        (4, 2, 3), (4, 2, 3), (4, 2), (4, 2), (4, 2), (2,), (2,), (2, 4), (4,), (4,), (2, 3, 3), (2, 3, 3), (3,), (3,),
        (3,), (3,), (3,),
    ]
    out = [
        jax.ShapeDtypeStruct((2, GROUP, BLOCK), BF16),
        jax.ShapeDtypeStruct((2, ROWS, 2 * HALF), BF16),
        jax.ShapeDtypeStruct((STRIPE, BLOCK), BF16),
    ]
    results = pl.pallas_call(
        functools.partial(kernel, scale),
        out_shape=out,
        in_specs=[pl.BlockSpec(memory_space=pl.ANY)] * 3,
        out_specs=[pl.BlockSpec(memory_space=pl.ANY)] * 3,
        scratch_shapes=[pltpu.VMEM(s, BF16) for s in vmem] + [dma(s) if s else dma for s in sems],
        compiler_params=pltpu.CompilerParams(
            collective_id=0, has_side_effects=True, vmem_limit_bytes=62 * 2**20
        ),
        cost_estimate=pl.CostEstimate(flops=29 * 10**9, bytes_accessed=8 * 2**20, transcendentals=0),
    )(inputs, weight, cotangent)
    return pl.pallas_call(
        hand_on,
        out_shape=out,
        in_specs=[pl.BlockSpec(memory_space=pl.ANY)] * 3,
        out_specs=[pl.BlockSpec(memory_space=pl.ANY)] * 3,
        scratch_shapes=[pltpu.VMEM(o.shape, BF16) for o in out] + [dma((7,)), dma((7,))],
        compiler_params=pltpu.CompilerParams(vmem_limit_bytes=62 * 2**20),
    )(*results)


def solution(mesh):
    return jax.shard_map(
        body,
        mesh=mesh,
        in_specs=(P(None, ("node", "local"), None), P("node", "local"), P(None, "node", "local")),
        out_specs=(P(None, "node", "local"), P(None, ("node", "local"), None), P("node", "local")),
        check_vma=False,
    )
```

```python
import functools
import math

import jax
import jax.numpy as jnp
from jax import lax
from jax.experimental import pallas as pl
from jax.experimental.pallas import tpu as pltpu
from jax.sharding import PartitionSpec as P

MESH = pl.DeviceIdType.MESH
F32 = jnp.float32
BF16 = jnp.bfloat16
NX = 4
ROWS = 64
STRIPE = 384
BLOCK = 768
GROUP = 512
HALF = 3072
WIDE = 1536
UNIT = 768
TILE = 256
FAR, BEFORE, OWN, AFTER = range(4)
FIRST = [(0, FAR), (1, FAR), (0, BEFORE), (1, AFTER)]
SECOND = [(1, BEFORE), (0, AFTER), (0, OWN), (1, OWN)]


def kernel(
    scale, x_ref, w_ref, c_ref, y_out, dx_out, dw_out,
    xg, wg, cg, dxp, fx, nx, dxf, ysend, yrecv, yfin, dwp, dwr, fy, ny, osnd, orcv, dwf,
    xloc, zx_s, zx_r, cloc, c_s, c_r, wloc, wd_s, wd_r, wo_s, wo_r, xr_s, xr_r, yr_s, yr_r, sib_s, sib_r,
    dx_s, dx_r, dxz_s, dxz_r, dxl, yy_s, yy_r, yl, dws_s, dws_r, dy_s, dy_r, do_s, do_r, dd_s, dd_r, ddl,
):
    node, local = lax.axis_index("node"), lax.axis_index("local")
    x, l = local // 2, local % 2
    y, h, c = node // 4, (node // 2) % 2, node % 2
    t = (l + h) % 2
    lw = (c + h) % 2
    keeps = c == t
    mine = jnp.where(keeps, 0, 1)

    def dev(x_, y_, h_, l_, c_):
        return ((y_ * 2 + h_) * 2 + c_, x_ * 2 + l_)

    def turn(v, by):
        return lax.rem(v + by + NX, NX)

    zp = dev(x, y, h, 1 - l, c)
    sib = dev(x, y, h, l, 1 - c)
    diag = dev(x, y, h, 1 - l, 1 - c)
    outer = dev(x, y, 1 - h, 1 - l, 1 - c)
    step = (1, -1)
    xn = [dev(turn(x, s), y, h, l, c) for s in step]
    yn = [dev(x, turn(y, s), h, l, c) for s in step]

    def remote(src, dst, ssem, rsem, to):
        return pltpu.make_async_remote_copy(
            src_ref=src, dst_ref=dst, send_sem=ssem, recv_sem=rsem, device_id=to, device_id_type=MESH
        )

    def at(start, size):
        return pl.ds(pl.multiple_of(start, size), size)

    def third(q):
        return slice(q * TILE, (q + 1) * TILE)

    def half(q):
        return slice(q * STRIPE, (q + 1) * STRIPE)

    lo = at(l * BLOCK, BLOCK)
    lz = at((1 - l) * BLOCK, BLOCK)
    lwc = at(lw * BLOCK, BLOCK)
    lwz = at((1 - lw) * BLOCK, BLOCK)

    def before(d):
        return BEFORE if d == 0 else AFTER

    def ahead(d):
        return AFTER if d == 0 else BEFORE

    def piece(d, k):
        return d if k != 1 else 1 - d

    def own_rows(rel):
        return at((l if rel == 0 else 1 - l) * ROWS, ROWS)

    def columns(v, e):
        return slice(v * UNIT + e * STRIPE, v * UNIT + (e + 1) * STRIPE)

    def stripe_columns(v, e, t_):
        return at(((turn(y, v - OWN) * 2 + e) * 2 + t_) * STRIPE, STRIPE)

    def x_local(v, e):
        return pltpu.make_async_copy(
            x_ref.at[:, :, stripe_columns(v, e, t)], xg.at[:, OWN, own_rows(0), columns(v, e)], xloc.at[v, e]
        )

    def x_swap(v, e, rel):
        return remote(
            x_ref.at[:, :, stripe_columns(v, e, 1 - t)], xg.at[:, OWN, own_rows(rel), columns(v, e)],
            zx_s.at[v, e], zx_r.at[v, e], zp,
        )

    def x_ring(rel, d, k):
        src, dst = (OWN, before(d)) if k < 2 else (before(d), FAR)
        m = piece(d, k)
        return remote(
            xg.at[m, src, own_rows(rel)], xg.at[m, dst, own_rows(rel)],
            xr_s.at[rel, d, k], xr_r.at[rel, d, k], xn[d],
        )

    def e_of(rel):
        return h if rel == 0 else 1 - h

    def w_part(v, e, cols):
        return wg.at[at(v * UNIT + e * STRIPE, STRIPE), cols]

    def w_local():
        return pltpu.make_async_copy(w_ref, w_part(OWN, h, lwc), wloc)

    def w_diag(cols):
        return remote(w_ref, w_part(OWN, h, cols), wd_s, wd_r, diag)

    def w_outer(rel):
        part = w_part(OWN, e_of(rel), lwc)
        return remote(part, part, wo_s, wo_r, outer)

    def w_ring(rel, d, k):
        src, dst = (OWN, before(d)) if k < 2 else (before(d), FAR)
        src, dst = [
            wg.at[at(v * UNIT + e_of(rel) * STRIPE + piece(d, k) * (STRIPE // 2), STRIPE // 2), lwc] for v in (src, dst)
        ]
        return remote(src, dst, yr_s.at[rel, d, k], yr_r.at[rel, d, k], yn[d])

    def w_sib(v, rel, cols):
        part = w_part(v, e_of(rel), cols)
        return remote(part, part, sib_s.at[v, rel], sib_r.at[v, rel], sib)

    def c_rows(m, s):
        return c_ref.at[m, at(turn(x, s - OWN) * (2 * ROWS), 2 * ROWS)]

    def c_local(m, s):
        return pltpu.make_async_copy(c_rows(m, s), cg.at[m, s, :, lo], cloc.at[m, s])

    def c_swap(m, s, cols):
        return remote(c_rows(m, s), cg.at[m, s, :, cols], c_s.at[m, s], c_r.at[m, s], zp)

    def dx_ring(v, d, k):
        ks = at(v * UNIT, UNIT)
        m = piece(d, k)
        src = dxp.at[m, FAR if k == 0 else ahead(d), :, ks]
        dst = fx.at[d, :, ks] if k == 0 else nx.at[d, m, :, ks]
        return remote(src, dst, dx_s.at[v, d, k], dx_r.at[v, d, k], xn[d])

    def dx_back(v, e, t_, mine):
        src = dxf.at[:, own_rows(0 if mine else 1), at(v * UNIT + e * STRIPE, STRIPE)]
        dst = dx_out.at[:, :, stripe_columns(v, e, t_)]
        if mine:
            return pltpu.make_async_copy(src, dst, dxl.at[v, e])
        return remote(src, dst, dxz_s.at[v, e], dxz_r.at[v, e], zp)

    def y_swap(m):
        return remote(ysend.at[m], yrecv.at[m], yy_s.at[m], yy_r.at[m], zp)

    def y_store(m, s):
        return pltpu.make_async_copy(
            yfin.at[m, s], y_out.at[m, at(turn(x, s - OWN) * (2 * ROWS), 2 * ROWS)], yl.at[m, s]
        )

    def dw_sib(v):
        rows = at(v * UNIT, UNIT)
        return remote(dwp.at[1, rows], dwr.at[rows], dws_s.at[v], dws_r.at[v], sib)

    def dw_rows(v, e):
        return at(v * UNIT + e * STRIPE, STRIPE)

    def dw_ring(d, k, q):
        p = piece(d, k)
        src = dwp.at[0, dw_rows(FAR if k == 0 else ahead(d), p), third(q)]
        dst = fy.at[d, :, third(q)] if k == 0 else ny.at[d, half(p), third(q)]
        return remote(src, dst, dy_s.at[d, k, q], dy_r.at[d, k, q], yn[d])

    def dw_outer(q):
        return remote(osnd.at[:, third(q)], orcv.at[:, third(q)], do_s.at[q], do_r.at[q], outer)

    def dw_diag(q):
        return remote(dwf.at[:, third(q)], dw_out.at[:, third(q)], dd_s.at[q], dd_r.at[q], diag)

    def dw_local(q):
        return pltpu.make_async_copy(dwf.at[:, third(q)], dw_out.at[:, third(q)], ddl.at[q])

    def y_tile(m, off, j):
        cols = at(off * BLOCK + j * TILE, TILE)
        return jnp.dot(xg[m].reshape(GROUP, HALF), wg[:, cols], preferred_element_type=F32).reshape(4, 2 * ROWS, TILE)

    def dx_rows(v, parts):
        @pl.loop(0, UNIT // TILE)
        def _(j):
            ks = at(v * UNIT + j * TILE, TILE)
            acc = lax.dot_general(
                jnp.concatenate([cg[m, s] for m, s in parts], axis=0), wg[ks, :], (((1,), (1,)), ((), ())),
                preferred_element_type=F32,
            )
            for i, (m, s) in enumerate(parts):
                dxp[m, s, :, ks] = acc[i * 2 * ROWS : (i + 1) * 2 * ROWS].astype(BF16)

    def dx_first(v):
        dx_rows(v, FIRST)
        for k in (0, 1):
            for d in (0, 1):
                dx_ring(v, d, k).start()

    def dx_relay(v):
        ks = at(v * UNIT, UNIT)
        for d in (0, 1):
            dx_ring(v, d, 0).wait_recv()
            dxp[d, ahead(d), :, ks] = (dxp[d, ahead(d), :, ks].astype(F32) + fx[d, :, ks].astype(F32)).astype(BF16)
            dx_ring(v, d, 2).start()

    def dx_final(v):
        ks = at(v * UNIT, UNIT)
        for k in (1, 2):
            for d in (0, 1):
                dx_ring(v, d, k).wait_recv()
        for m in (0, 1):
            dxf[m, :, ks] = (
                dxp[m, OWN, :, ks].astype(F32) + nx[0, m, :, ks].astype(F32) + nx[1, m, :, ks].astype(F32)
            ).astype(BF16)
        for e in (0, 1):
            dx_back(v, e, t, False).start()
            dx_back(v, e, t, True).start()

    def dw_block(v, own):
        off = (l if own else 1 - l) * BLOCK
        slot = mine if own else 1 - mine

        @pl.loop(0, UNIT // TILE)
        def _(j):
            ks = at(v * UNIT + j * TILE, TILE)
            xt = xg[:, :, :, ks].reshape(2 * GROUP, TILE).T
            for n in range(BLOCK // TILE):
                cv = cg[:, :, :, at(off + n * TILE, TILE)].reshape(2 * GROUP, TILE)
                acc = jnp.dot(xt, cv, preferred_element_type=F32)
                dwp[slot, ks, n * TILE : (n + 1) * TILE] = (acc * scale).astype(BF16)

        @pl.when(jnp.logical_not(keeps) if own else keeps)
        def _():
            dw_sib(v).start()

    def dw_merge(v):
        dw_sib(v).wait_recv()

        @pl.loop(0, 4)
        def _(j):
            part = at(v * UNIT + j * (UNIT // 4), UNIT // 4)
            dwp[0, part, :] = (dwp[0, part, :].astype(F32) + dwr[part, :].astype(F32)).astype(BF16)

    def dw_send_far():
        for q in range(3):
            for d in (0, 1):
                dw_ring(d, 0, q).start()

    def dw_send_near(d):
        for q in range(3):
            dw_ring(d, 1, q).start()

    def dw_relay(q):
        for d in (0, 1):
            dw_ring(d, 0, q).wait_recv()
            rows = dw_rows(ahead(d), d)
            dwp[0, rows, third(q)] = (dwp[0, rows, third(q)].astype(F32) + fy[d, :, third(q)].astype(F32)).astype(BF16)
            dw_ring(d, 2, q).start()

    def dw_total(e, q):
        rows = at(e * STRIPE, STRIPE)
        return (
            dwp[0, dw_rows(OWN, e), third(q)].astype(F32)
            + ny[0, rows, third(q)].astype(F32)
            + ny[1, rows, third(q)].astype(F32)
        )

    stripes = [(v, e) for v in range(4) for e in range(2)]
    both = (0, 1)
    for v, e in stripes:
        x_local(v, e).start()
    for m, s in FIRST + SECOND:
        c_local(m, s).start()

    @pl.when(keeps)
    def _():
        w_local().start()

    barrier = pltpu.get_barrier_semaphore()
    friends = [zp, sib, diag, outer, *xn, *yn]
    for friend in friends:
        pl.semaphore_signal(barrier, inc=1, device_id=friend, device_id_type=MESH)
    pl.semaphore_wait(barrier, len(friends))

    @pl.when(jnp.logical_not(keeps))
    def _():
        w_diag(lo).start()

    for v, e in stripes:
        x_swap(v, e, 0).start()

    def c_start():
        for m, s in FIRST + SECOND:
            c_swap(m, s, lo).start()

    pl.when(jnp.logical_not(keeps))(c_start)

    for v, e in stripes:
        x_local(v, e).wait()
    for k in both:
        for d in both:
            x_ring(0, d, k).start()

    @pl.when(keeps)
    def _():
        w_local().wait()

    @pl.when(jnp.logical_not(keeps))
    def _():
        w_diag(lo).wait_send()
        w_diag(lwc).wait_recv()

    w_outer(0).start()
    for k in both:
        for d in both:
            w_ring(0, d, k).start()
    w_sib(OWN, 0, lwc).start()

    for d in both:
        x_ring(0, d, 0).wait_recv()
        x_ring(0, d, 2).start()
    for d in both:
        w_ring(0, d, 0).wait_recv()
        w_ring(0, d, 2).start()
    w_outer(1).wait_recv()
    for k in both:
        for d in both:
            w_ring(1, d, k).start()
    w_sib(OWN, 1, lwc).start()
    for v, e in stripes:
        x_swap(v, e, 1).wait_recv()
    for k in both:
        for d in both:
            x_ring(1, d, k).start()
    pl.when(keeps)(c_start)
    for d in both:
        w_ring(0, d, 1).wait_recv()
        w_sib(before(d), 0, lwc).start()
    for d in both:
        w_ring(0, d, 2).wait_recv()
    w_sib(FAR, 0, lwc).start()
    for d in both:
        w_ring(1, d, 0).wait_recv()
        w_ring(1, d, 2).start()
    for d in both:
        x_ring(1, d, 0).wait_recv()
        x_ring(1, d, 2).start()
    for d in both:
        w_ring(1, d, 1).wait_recv()
        w_sib(before(d), 1, lwc).start()

    def w_arrived(v):
        for rel in both:
            w_sib(v, rel, lwz).wait_recv()

    for m, s in FIRST + SECOND:
        c_local(m, s).wait()
    for m, s in FIRST:
        c_swap(m, s, lz).wait_recv()
    w_arrived(OWN)
    w_arrived(AFTER)
    w_arrived(BEFORE)

    @pl.loop(0, 3)
    def _(i):
        dx_first(jnp.where(i == 0, OWN, jnp.where(i == 1, AFTER, BEFORE)))

    for d in both:
        w_ring(1, d, 2).wait_recv()
    w_sib(FAR, 1, lwc).start()
    w_arrived(FAR)
    dx_first(FAR)
    for rel in both:
        for d in both:
            for k in (1, 2):
                x_ring(rel, d, k).wait_recv()

    def y_first(m):
        @pl.loop(0, BLOCK // TILE)
        def _(j):
            ysend[m, :, :, at(j * TILE, TILE)] = y_tile(m, 1 - l, j).astype(BF16)

        y_swap(m).start()

    y_first(0)
    dw_block(FAR, True)
    dw_block(AFTER, True)

    @pl.when(keeps)
    def _():
        dw_merge(FAR)
        dw_send_far()

    dw_block(BEFORE, True)

    @pl.when(keeps)
    def _():
        dw_merge(AFTER)
        dw_send_near(0)

    y_first(1)

    @pl.when(keeps)
    def _():
        dw_merge(BEFORE)
        dw_send_near(1)

    dw_block(OWN, True)

    @pl.when(keeps)
    def _():
        dw_merge(OWN)

    for m, s in SECOND:
        c_swap(m, s, lz).wait_recv()
    sends = jnp.logical_not(keeps)

    @pl.loop(0, 3)
    def _(i):
        dw_block(jnp.where(i == 0, FAR, jnp.where(i == 1, AFTER, BEFORE)), False)

        @pl.when(keeps & (i == 0))
        def _():
            for q in range(3):
                dw_relay(q)

        @pl.when(sends & (i == 1))
        def _():
            dw_merge(FAR)
            dw_send_far()

        @pl.when(sends & (i == 2))
        def _():
            dw_merge(AFTER)
            dw_send_near(0)

    @pl.loop(0, 4)
    def _(i):
        v = jnp.where(i == 0, OWN, jnp.where(i == 1, AFTER, jnp.where(i == 2, BEFORE, FAR)))

        @pl.when(i == 3)
        def _():
            dw_block(OWN, False)

        dx_rows(v, SECOND)

        @pl.when(sends & (i == 0))
        def _():
            dw_merge(BEFORE)
            dw_send_near(1)

        dx_relay(v)

        @pl.when(sends & (i == 1))
        def _():
            for q in range(3):
                dw_relay(q)

        @pl.when(sends & (i == 3))
        def _():
            dw_merge(OWN)

    def y_second(m):
        y_swap(m).wait_recv()

        @pl.loop(0, BLOCK // TILE)
        def _(j):
            js = at(j * TILE, TILE)
            yfin[m, :, :, js] = (y_tile(m, l, j) + yrecv[m, :, :, js].astype(F32)).astype(BF16)

        for s in range(4):
            y_store(m, s).start()

    dx_final(OWN)
    dx_final(AFTER)
    for q in range(3):
        for d in both:
            for k in (1, 2):
                dw_ring(d, k, q).wait_recv()
        osnd[:, third(q)] = dw_total(1 - h, q).astype(BF16)
        dw_outer(q).start()
    dx_final(BEFORE)
    dx_final(FAR)
    for q in range(3):
        dw_outer(q).wait_recv()
        dwf[:, third(q)] = (dw_total(h, q) + orcv[:, third(q)].astype(F32)).astype(BF16)

        @pl.when(keeps)
        def _():
            dw_local(q).start()

        @pl.when(jnp.logical_not(keeps))
        def _():
            dw_diag(q).start()

    y_second(0)
    y_second(1)

    for q in range(3):

        @pl.when(keeps)
        def _():
            dw_local(q).wait()

        @pl.when(jnp.logical_not(keeps))
        def _():
            dw_diag(q).wait()

    for v in range(4):
        for rel in both:
            w_sib(v, rel, lwc).wait_send()
    w_outer(0).wait_send()
    for v, e in stripes:
        x_swap(v, e, 0).wait_send()
    for m, s in FIRST + SECOND:
        c_swap(m, s, lo).wait_send()
    for rel in both:
        for d in both:
            for k in range(3):
                x_ring(rel, d, k).wait_send()
                w_ring(rel, d, k).wait_send()
    for q in range(3):
        for d in both:
            for k in range(3):
                dw_ring(d, k, q).wait_send()
        dw_outer(q).wait_send()
    for m in both:
        y_swap(m).wait_send()
        for s in range(4):
            y_store(m, s).wait()

    @pl.loop(0, 4)
    def _(v):
        dw_sib(v).wait_send()
        for d in both:
            for k in range(3):
                dx_ring(v, d, k).wait_send()
        for e in both:
            dx_back(v, e, t, False).wait_send()
            dx_back(v, e, 1 - t, False).wait_recv()
            dx_back(v, e, t, True).wait()


def hand_on(y_ref, dx_ref, dw_ref, y_out, dx_out, dw_out, y_buf, dx_buf, dw_buf, sem_in, sem_out):
    pieces = []
    for m in range(2):
        for i in range(2):
            pieces.append((y_ref, y_buf, y_out, (m, pl.ds(i * GROUP // 2, GROUP // 2))))
        pieces.append((dx_ref, dx_buf, dx_out, (m,)))
    pieces.append((dw_ref, dw_buf, dw_out, (pl.ds(0, STRIPE),)))
    loads = [pltpu.make_async_copy(a.at[i], b.at[i], sem_in.at[k]) for k, (a, b, _, i) in enumerate(pieces)]
    stores = [pltpu.make_async_copy(b.at[i], o.at[i], sem_out.at[k]) for k, (_, b, o, i) in enumerate(pieces)]
    for load in loads:
        load.start()
    for load, store in zip(loads, stores):
        load.wait()
        store.start()
    for store in stores:
        store.wait()


def body(inputs, weight, cotangent):
    scale = 1.0 / math.sqrt(
        inputs.shape[0] * inputs.shape[1] * lax.axis_size("node") * lax.axis_size("local")
    )
    dma = pltpu.SemaphoreType.DMA
    vmem = [
        (2, 4, 2 * ROWS, HALF), (HALF, WIDE), (2, 4, 2 * ROWS, WIDE),
        (2, 4, 2 * ROWS, HALF), (2, 2 * ROWS, HALF), (2, 2, 2 * ROWS, HALF), (2, 2 * ROWS, HALF),
        (2, 4, 2 * ROWS, BLOCK), (2, 4, 2 * ROWS, BLOCK), (2, 4, 2 * ROWS, BLOCK),
        (2, HALF, BLOCK), (HALF, BLOCK),
        (2, STRIPE, BLOCK), (2, UNIT, BLOCK), (STRIPE, BLOCK), (STRIPE, BLOCK), (STRIPE, BLOCK),
    ]
    sems = [
        (4, 2), (4, 2), (4, 2), (2, 4), (2, 4), (2, 4), (), (), (), (), (), (2, 2, 3), (2, 2, 3), (2, 2, 3), (2, 2, 3), (4, 2), (4, 2),
        (4, 2, 3), (4, 2, 3), (4, 2), (4, 2), (4, 2), (2,), (2,), (2, 4), (4,), (4,), (2, 3, 3), (2, 3, 3), (3,), (3,),
        (3,), (3,), (3,),
    ]
    out = [
        jax.ShapeDtypeStruct((2, GROUP, BLOCK), BF16),
        jax.ShapeDtypeStruct((2, ROWS, 2 * HALF), BF16),
        jax.ShapeDtypeStruct((STRIPE, BLOCK), BF16),
    ]
    results = pl.pallas_call(
        functools.partial(kernel, scale),
        out_shape=out,
        in_specs=[pl.BlockSpec(memory_space=pl.ANY)] * 3,
        out_specs=[pl.BlockSpec(memory_space=pl.ANY)] * 3,
        scratch_shapes=[pltpu.VMEM(s, BF16) for s in vmem] + [dma(s) if s else dma for s in sems],
        compiler_params=pltpu.CompilerParams(
            collective_id=0, has_side_effects=True, vmem_limit_bytes=62 * 2**20
        ),
        cost_estimate=pl.CostEstimate(flops=29 * 10**9, bytes_accessed=8 * 2**20, transcendentals=0),
    )(inputs, weight, cotangent)
    return pl.pallas_call(
        hand_on,
        out_shape=out,
        in_specs=[pl.BlockSpec(memory_space=pl.ANY)] * 3,
        out_specs=[pl.BlockSpec(memory_space=pl.ANY)] * 3,
        scratch_shapes=[pltpu.VMEM(o.shape, BF16) for o in out] + [dma((7,)), dma((7,))],
        compiler_params=pltpu.CompilerParams(vmem_limit_bytes=62 * 2**20),
    )(*results)


def solution(mesh):
    return jax.shard_map(
        body,
        mesh=mesh,
        in_specs=(P(None, ("node", "local"), None), P("node", "local"), P(None, "node", "local")),
        out_specs=(P(None, "node", "local"), P(None, ("node", "local"), None), P("node", "local")),
        check_vma=False,
    )
```
